256 devices in a mesh: row: 32 (over y, z), col: 8 (over x, core).
Axes of the slice: x: 4, y: 4, z: 8, core: 2. Of those that a mesh axis runs over, the one named last changes fastest.
Arguments:
- features: float32 [16, 1024, 128], P(None, 'col'), may hold values from -6 to 6
- lengthscales: float32 [128], replicated, may hold values from 8 to 32
- noise_var: float32 [16, 1024], P(None, 'col'), may hold values from 0.5 to 2
- component: float32 [4, 4096, 16, 1024], P(None, 'row', None, 'col'), may hold values from 0 to 1, as said below
- step_index: int32 [1], replicated, may hold values from 0 to 126
Outputs:
- panel_factor: float32 [4, 4096, 128], P(None, 'row', 'col')
- trailing: float32 [4, 4096, 16, 1024], P(None, 'row', None, 'col')
The draws below stay inside these ranges and needn't reach their ends.
Inputs may be any that keep to these rules, and one draw needn't show every extreme that they name: component is symmetric and positive semi-definite with entries in [0, 1], so that covar is symmetric positive definite.
All inputs are finite; a program needn't handle non-finite values.
Results may differ from the reference program's by a relative error of at most 0.0003.
Values sent between devices are 32-bit elements; how exact they have to be, the bound alone decides.
A program may use at most 64 MiB of HBM per device.

```python
import math
import jax
import jax.numpy as jnp
from jax import lax

D = 128
B = 128
KR = 4
KC = 16
N_ROW = 32
N_COL = 8


def draw_component(key, part):
    key = jax.random.fold_in(key, 11)
    npts = KR * N_ROW * B
    stamps = jax.random.uniform(key, (npts,), jnp.float32)
    row_stamps = stamps.reshape(KR, N_ROW * B)
    col_stamps = stamps.reshape(KC, N_COL * B)
    spread = row_stamps[:, :, None, None] - col_stamps[None, None, :, :]
    return jnp.exp(-200.0 * (spread * spread))


def steps_of(stream_key, dims, split, low, top_value):
    loudness = 1.0
    for dim, shards_of in split:
        steps = jax.random.uniform(jax.random.fold_in(jax.random.fold_in(stream_key, 6), dim), (shards_of,), jnp.float32, low / len(split), top_value / len(split))
        loudness = loudness * jnp.repeat(jnp.exp(steps), dims[dim] // shards_of).reshape((-1,) + (1,) * (len(dims) - 1 - dim))
    return loudness


def noise(key, shape, scale, limit, shards=(), kind=jnp.bfloat16):
    array = scale * jax.random.normal(key, shape, jnp.float32)
    if shards:
        array = array * steps_of(key, shape, shards, -0.22, 0.18)
    return jnp.clip(array, -limit, limit).astype(kind)


def setup_inputs(seed: int = 0) -> dict:
    key_list = jax.random.split(jax.random.key(seed), 6)
    features = noise(key_list[0], (KC, N_COL * B, D), 1.0, 6.0, ((1, 8),), jnp.float32)
    lengthscales = jnp.clip(jnp.exp(jax.random.uniform(key_list[1], (D,), jnp.float32, math.log(8.0), math.log(32.0))), 8.0, 32.0)
    noise_var = jnp.clip(0.5 + 1.5 * jax.random.uniform(key_list[2], (KC, N_COL * B), jnp.float32) ** steps_of(key_list[2], (KC, N_COL * B), ((1, 8),), -0.2, 0.2), 0.5, 2.0)
    component = draw_component(jax.random.fold_in(key_list[5], 71), 0)
    step_index = jax.random.randint(key_list[4], (1,), 0, KR * N_ROW - 1).astype(jnp.int32)
    return {"features": features, "lengthscales": lengthscales, "noise_var": noise_var, "component": component, "step_index": step_index}


def kernel_block(left_points, left_squares, right_points, right_squares):
    inner = jnp.dot(left_points.astype(jnp.float32), right_points.T.astype(jnp.float32), precision=lax.Precision.HIGHEST, preferred_element_type=jnp.float32)
    distance = left_squares[:, None] + right_squares[None, :] - 2.0 * inner
    return jnp.exp(-0.5 * distance)

def reference(features, lengthscales, noise_var, component, step_index):
    npts = KR * N_ROW * B
    nblocks = KR * N_ROW
    points = features.reshape(npts, D) / lengthscales[None, :]
    squares = jnp.sum(points * points, axis=1)
    noise_all = noise_var.reshape(npts)
    prior_table = component.reshape(npts, npts)
    panel_index = step_index[0]
    first_row = (panel_index * B).astype(jnp.int32)
    point_ids = jnp.arange(npts, dtype=jnp.int32)
    panel_ids = first_row + jnp.arange(B, dtype=jnp.int32)
    panel_points = lax.dynamic_slice_in_dim(points, first_row, B, 0)
    panel_squares = lax.dynamic_slice_in_dim(squares, first_row, B, 0)
    panel_noise = lax.dynamic_slice_in_dim(noise_all, first_row, B, 0)
    column_kernel = kernel_block(points, squares, panel_points, panel_squares)
    column_table = lax.dynamic_slice_in_dim(prior_table, first_row, B, 1)
    same = point_ids[:, None] == panel_ids[None, :]
    column_tiles = column_kernel + column_table + jnp.where(same, panel_noise[None, :], 0.0)
    diagonal = lax.dynamic_slice_in_dim(column_tiles, first_row, B, 0)
    factor = jnp.linalg.cholesky(diagonal)
    solved = lax.linalg.triangular_solve(factor, column_tiles.T, left_side=True, lower=True).T
    blocks = point_ids // B
    repeated = jnp.tile(factor, (nblocks, 1))
    panel_factor = jnp.where((blocks < panel_index)[:, None], 0.0, jnp.where((blocks == panel_index)[:, None], repeated, solved))
    masked = jnp.where((blocks > panel_index)[:, None], solved, 0.0)

    def one_block(block):
        start = (block * B).astype(jnp.int32)
        row_points = lax.dynamic_slice_in_dim(points, start, B, 0)
        row_squares = lax.dynamic_slice_in_dim(squares, start, B, 0)
        kernel = kernel_block(row_points, row_squares, points, squares)
        table_rows = lax.dynamic_slice_in_dim(prior_table, start, B, 0)
        row_ids = start + jnp.arange(B, dtype=jnp.int32)
        added = jnp.where(row_ids[:, None] == point_ids[None, :], noise_all[None, :], 0.0)
        masked_rows = lax.dynamic_slice_in_dim(masked, start, B, 0)
        update = jnp.dot(masked_rows.astype(jnp.float32), masked.T.astype(jnp.float32), precision=lax.Precision.HIGHEST, preferred_element_type=jnp.float32)
        return kernel + table_rows + added - update
    trailing = lax.map(one_block, jnp.arange(nblocks, dtype=jnp.int32)).reshape(npts, npts)
    return (panel_factor.reshape(KR, N_ROW * B, B), trailing.reshape(KR, N_ROW * B, KC, N_COL * B))
```

```python
import functools

import jax
import jax.numpy as jnp
from jax import lax
from jax.experimental import pallas as pl
from jax.experimental.pallas import tpu as pltpu
from jax.sharding import PartitionSpec as P

MESH = pl.DeviceIdType.MESH
F32 = jnp.float32
BF16 = jnp.bfloat16
B = 128
KR, KC, NR, NC = 4, 16, 32, 8
NY, NZ = 4, 8
PART = B // NC
PANEL = KR * PART
XROWS = PANEL + PART + 8
VMEM_LIMIT = 56 * 1024 * 1024


def split3(x):
    high = x.astype(BF16)
    rest = x - high.astype(F32)
    mid = rest.astype(BF16)
    low = (rest - mid.astype(F32)).astype(BF16)
    return high, mid, low


def left6(x, axis=1):
    h, m, l = split3(x)
    return jnp.concatenate([h, h, m, h, m, l], axis=axis)


def right6(x, axis=1):
    h, m, l = split3(x)
    return jnp.concatenate([h, m, h, l, m, h], axis=axis)


def dot_nt(a, b):
    return lax.dot_general(a, b, (((1,), (1,)), ((), ())), preferred_element_type=F32)


def lane_squares(points):
    cat = jnp.concatenate(split3(points * points), axis=1)
    ones = jnp.ones((16, cat.shape[1]), BF16)
    return dot_nt(ones, cat)[0:8, :]


def factor_inverse(w_ref, dv_ref):
    size = 16
    lane = lax.broadcasted_iota(jnp.int32, (size, B), 1)
    row = lax.broadcasted_iota(jnp.int32, (size, B), 0)

    def block(b, carry):
        start = pl.multiple_of(b * size, size)
        rows = pl.ds(start, size)
        left = w_ref[rows, 0:B]
        right = w_ref[rows, B : 2 * B]
        rolled = pltpu.roll(left, lax.rem(B - start, B), axis=1)
        cols = [jnp.broadcast_to(rolled[:, k : k + 1], (size, B)) for k in range(size)]
        inv = jnp.zeros((size, B), F32)
        for k in range(size):
            pivot = jnp.broadcast_to(cols[k][k : k + 1, :], (size, B))
            rinv = 1.0 / pivot
            inv = jnp.where(row == k, rinv, inv)
            mult = jnp.where(row > k, cols[k] * rinv, 0.0)
            for j in range(k + 1, size):
                cols[j] = cols[j] - mult * cols[j][k : k + 1, :]
            left = left - mult * left[k : k + 1, :]
            right = right - mult * right[k : k + 1, :]
        w_ref[rows, 0:B] = left
        w_ref[rows, B : 2 * B] = right
        dv_ref[rows, :] = inv
        scaled = jnp.where(lane >= start + size, left * inv, 0.0)
        update = lax.dot_general(
            left6(scaled, 0),
            right6(jnp.concatenate([left, right], axis=1), 0),
            (((0,), (0,)), ((), ())),
            preferred_element_type=F32,
        )
        w_ref[...] = w_ref[...] - update
        return carry

    lax.fori_loop(0, B // size, block, 0)
    return w_ref[:, B : 2 * B] * jnp.sqrt(dv_ref[...])


def gather_kernel(
    step_ref,
    feat_ref,
    ls_ref,
    noise_ref,
    comp_ref,
    covar_ref,
    linv_ref,
    rowc_ref,
    colc_ref,
    comp_v,
    feat_v,
    s_a,
    r_a,
    z_a,
    y_a,
    diag,
    s_b,
    r_b,
    g_b,
    colall,
    rowfeat,
    colcat,
    rowcat,
    sqcol,
    covar_v,
    w_v,
    dv_v,
    local_sem,
    send_sem,
    recv_sem,
):
    r = lax.axis_index("row")
    c = lax.axis_index("col")
    z = lax.rem(r, NZ)
    y = lax.div(r, NZ)

    def at_x(i):
        return (r, i)

    def at_z(i):
        return (y * NZ + i, c)

    def at_y(i):
        return (i * NZ + z, c)

    partner = (y * NZ + c, z)

    def other(me, d, n):
        return lax.rem(me + d, n)

    feat_copy = pltpu.make_async_copy(feat_ref, feat_v, local_sem.at[0])
    comp_copy = pltpu.make_async_copy(comp_ref, comp_v, local_sem.at[1])
    comp_copy.start()
    feat_copy.start()

    barrier = pltpu.get_barrier_semaphore()
    for d in range(1, NC):
        pl.semaphore_signal(barrier, inc=1, device_id=at_x(other(c, d, NC)), device_id_type=MESH)
    for d in range(1, NZ):
        pl.semaphore_signal(barrier, inc=1, device_id=at_z(other(z, d, NZ)), device_id_type=MESH)
    for d in range(1, NY):
        pl.semaphore_signal(barrier, inc=1, device_id=at_y(other(y, d, NY)), device_id_type=MESH)

    @pl.when(z != c)
    def _():
        pl.semaphore_signal(barrier, inc=1, device_id=partner, device_id_type=MESH)

    def remote(src, dst, slot, recv, dev):
        return pltpu.make_async_remote_copy(
            src_ref=src,
            dst_ref=dst,
            send_sem=send_sem.at[slot],
            recv_sem=recv_sem.at[recv],
            device_id=dev,
            device_id_type=MESH,
        )

    waits = []

    def spread(src, dst, off, n, me, dev):
        for d in range(1, n):
            peer = other(me, d, n)
            copy = remote(src(peer), dst(me), off + d, off + me, dev(peer))
            copy.start()
            waits.append(copy)

    def arrived(dst, off, n, me, dev):
        for d in range(1, n):
            peer = other(me, d, n)
            remote(dst(peer), dst(peer), off + d, off + peer, dev(peer)).wait_recv()

    p = step_ref[0]
    panel_m = lax.div(p, NC)
    panel_c = lax.rem(p, NC)
    panel_k = lax.div(p, NR)
    panel_r = lax.rem(p, NR)
    panel_z = lax.rem(panel_r, NZ)
    panel_y = lax.div(panel_r, NZ)
    inv_ls = 1.0 / ls_ref[...]

    comp_copy.wait()
    cand = comp_v[pl.ds(panel_k * (B * KC) + panel_m, B, stride=KC), :]
    s_a[...] = cand.reshape(NC, PART, B)
    for k in range(KR):
        block = comp_v[pl.ds(k * (B * KC) + panel_m, B, stride=KC), :]
        s_b[:, k * PART : (k + 1) * PART, :] = block.reshape(NC, PART, B)
    feat_copy.wait()
    feat_p = feat_v[lax.div(panel_m, 4), lax.rem(panel_m, 4)] * inv_ls
    s_b[:, PANEL : PANEL + PART, :] = feat_p.reshape(NC, PART, B)
    noise_p = noise_ref[pl.ds(panel_m, 1), :]
    s_b[:, PANEL + PART : XROWS, :] = jnp.broadcast_to(noise_p.reshape(1, 1, B), (NC, 8, B))
    r_a[c] = s_a[c]
    r_b[c] = s_b[c]

    @pl.when(z != c)
    def _():
        pl.semaphore_wait(barrier, 2 * NC + NY - 2)

    @pl.when(z == c)
    def _():
        pl.semaphore_wait(barrier, 2 * NC + NY - 3)

    spread(lambda i: s_a.at[i], lambda i: r_a.at[i], 0, NC, c, at_x)
    spread(lambda i: s_b.at[i], lambda i: r_b.at[i], 8, NC, c, at_x)

    feat_move = [remote(feat_v.at[k, y], rowfeat.at[k], 80 + k, 80 + k, partner) for k in range(KR)]

    @pl.when(z != c)
    def _():
        for copy in feat_move:
            copy.start()

    @pl.when(z == c)
    def _():
        for k in range(KR):
            rowfeat[k] = feat_v[k, y]

    def prepare(m, carry):
        pts = feat_v[lax.div(m, 4), lax.rem(m, 4)] * inv_ls
        colcat[pl.ds(pl.multiple_of(m * B, B), B), :] = right6(pts)
        sqcol[m] = lane_squares(pts)
        return carry

    arrived(lambda i: r_a.at[i], 0, NC, c, at_x)
    z_a[z] = r_a[panel_c]
    spread(lambda i: z_a.at[z], lambda i: z_a.at[i], 16, NZ, z, at_z)
    lax.fori_loop(0, KC // 2, prepare, 0)

    arrived(lambda i: r_b.at[i], 8, NC, c, at_x)
    g_b[c] = r_b[panel_c]
    move = remote(g_b.at[c, 0:PANEL], colall.at[y, c], 24, 24, partner)
    moved = remote(g_b.at[c, 0:PANEL], colall.at[y, z], 24, 24, partner)

    @pl.when(z != c)
    def _():
        move.start()

    @pl.when(z == c)
    def _():
        colall[y, z] = g_b[c, 0:PANEL, :]

    spread(lambda i: g_b.at[c], lambda i: g_b.at[i], 32, NC, c, at_x)

    arrived(lambda i: z_a.at[i], 16, NZ, z, at_z)
    y_a[y] = z_a[panel_z]
    spread(lambda i: y_a.at[y], lambda i: y_a.at[i], 40, NY, y, at_y)

    @pl.when(z != c)
    def _():
        moved.wait_recv()

    spread(lambda i: colall.at[y, z], lambda i: colall.at[y, i], 48, NZ, z, at_z)
    lax.fori_loop(KC // 2, KC, prepare, 0)

    arrived(lambda i: y_a.at[i], 40, NY, y, at_y)
    diag[c] = y_a[panel_y]
    spread(lambda i: diag.at[c], lambda i: diag.at[i], 56, NC, c, at_x)

    arrived(lambda i: colall.at[y, i], 48, NZ, z, at_z)
    spread(lambda i: colall.at[y], lambda i: colall.at[i], 64, NY, y, at_y)

    @pl.when(z != c)
    def _():
        for copy in feat_move:
            copy.wait_recv()

    half_row = []
    for k in range(KR):
        pts = rowfeat[k] * inv_ls
        rowcat[k * B : (k + 1) * B, :] = left6(pts)
        half_row.append(0.5 * jnp.sum(pts * pts, axis=1, keepdims=True))
    eye = lax.broadcasted_iota(jnp.int32, (B, B), 0) == lax.broadcasted_iota(jnp.int32, (B, B), 1)

    def cover(m2, carry):
        cols = colcat[pl.ds(pl.multiple_of(m2 * 2 * B, 2 * B), 2 * B), :]
        for k in range(KR):
            prod = dot_nt(rowcat[k * B : (k + 1) * B, :], cols)
            for j in range(2):
                m = m2 * 2 + j
                half_col = 0.5 * sqcol[m][0:1, :]
                expo = prod[:, j * B : (j + 1) * B] - (half_row[k] + half_col)
                value = jnp.exp(expo) + comp_v[pl.ds(k * (B * KC) + m, B, stride=KC), :]
                same = jnp.logical_and(z == c, m == k * 4 + y)
                added = jnp.where(jnp.logical_and(eye, same), noise_ref[pl.ds(m, 1), :], 0.0)
                covar_v[k * KC + m] = value + added
        return carry

    lax.fori_loop(0, KC // 2, cover, 0)
    covar_copy = pltpu.make_async_copy(covar_v, covar_ref, local_sem.at[2])
    covar_copy.start()

    arrived(lambda i: g_b.at[i], 32, NC, c, at_x)
    pts_p = g_b[:, PANEL : PANEL + PART, :].reshape(B, B)
    noise_full = g_b[0, PANEL + PART : PANEL + PART + 1, :]
    left_p, right_p = left6(pts_p), right6(pts_p)
    half_p = 0.5 * lane_squares(pts_p)[0:1, :]
    half_p_col = 0.5 * jnp.sum(pts_p * pts_p, axis=1, keepdims=True)
    kernel_p = jnp.exp(dot_nt(left_p, right_p) - (half_p_col + half_p))
    noise_p = jnp.where(eye, noise_full, 0.0)
    arrived(lambda i: diag.at[i], 56, NC, c, at_x)
    w_v[:, 0:B] = kernel_p + diag[...].reshape(B, B) + noise_p
    w_v[:, B : 2 * B] = jnp.where(eye, 1.0, 0.0)
    linv_ref[...] = factor_inverse(w_v, dv_v)

    for k in range(KR):
        kern = jnp.exp(dot_nt(rowcat[k * B : (k + 1) * B, :], right_p) - (half_row[k] + half_p))
        raw = g_b[:, k * PART : (k + 1) * PART, :].reshape(B, B)
        here = k * NR + r == p
        rowc_ref[k] = kern + raw + jnp.where(here, noise_p, 0.0)

    def column(m, carry):
        pts = feat_v[lax.div(m, 4), lax.rem(m, 4)] * inv_ls
        half = 0.5 * jnp.sum(pts * pts, axis=1, keepdims=True)
        cols = colcat[pl.ds(pl.multiple_of(m * B, B), B), :]
        colc_ref[m] = jnp.exp(dot_nt(cols, left_p) - (half + half_p))
        return carry

    lax.fori_loop(0, KC, column, 0)
    arrived(lambda i: colall.at[i], 64, NY, y, at_y)
    for m in range(KC):
        k, q = m // NY, m % NY
        colc_ref[m] = colc_ref[m] + colall[q, :, k * PART : (k + 1) * PART, :].reshape(B, B)

    covar_copy.wait()
    for copy in waits:
        copy.wait_send()

    @pl.when(z != c)
    def _():
        move.wait_send()
        for copy in feat_move:
            copy.wait_send()


def update_kernel(step_ref, linv_ref, rowc_ref, colc_ref, covar_ref, pf_ref, out_ref, srow, scol):
    r = lax.axis_index("row")
    c = lax.axis_index("col")
    p = step_ref[0]
    step = pl.program_id(0)

    @pl.when(step == 0)
    def _():
        inverse = right6(linv_ref[...])
        share = right6(linv_ref[pl.ds(pl.multiple_of(c * PART, PART), PART), :])
        row = lax.broadcasted_iota(jnp.int32, (PART, B), 1)
        col = lax.broadcasted_iota(jnp.int32, (PART, B), 0) + c * PART
        for k in range(KR):
            w = k * NR + r
            left = left6(rowc_ref[k])
            solved = jnp.where(w > p, dot_nt(left, inverse), 0.0)
            h, m, _ = split3(solved)
            srow[k * B : (k + 1) * B, :] = jnp.concatenate([h, h, m], axis=1)
            mine = dot_nt(share, left)
            keep = jnp.logical_or(w > p, jnp.logical_and(w == p, col <= row))
            pf_ref[k] = jnp.where(keep, mine, 0.0)

        def column(i, carry):
            u = i * NC + c
            solved = jnp.where(u > p, dot_nt(left6(colc_ref[i]), inverse), 0.0)
            h, m, _ = split3(solved)
            scol[pl.ds(pl.multiple_of(i * B, B), B), :] = jnp.concatenate([h, m, h], axis=1)
            return carry

        lax.fori_loop(0, KC, column, 0)

    rows = srow[pl.ds(pl.multiple_of(step * B, B), B), :]

    def pair(m2, carry):
        cols = scol[pl.ds(pl.multiple_of(m2 * 2 * B, 2 * B), 2 * B), :]
        update = dot_nt(rows, cols)
        for j in range(2):
            m = m2 * 2 + j
            out_ref[pl.ds(m, B, stride=KC), :] = covar_ref[m] - update[:, j * B : (j + 1) * B]
        return carry

    lax.fori_loop(0, KC // 2, pair, 0)


def body(features, lengthscales, noise_var, component, step_index):
    any_spec = pl.BlockSpec(memory_space=pl.ANY)
    vmem = pl.BlockSpec(memory_space=pltpu.VMEM)
    smem = pl.BlockSpec(memory_space=pltpu.SMEM)
    covar, linv, rowc, colc = pl.pallas_call(
        gather_kernel,
        out_shape=(
            jax.ShapeDtypeStruct((KR * KC, B, B), F32),
            jax.ShapeDtypeStruct((B, B), F32),
            jax.ShapeDtypeStruct((KR, B, B), F32),
            jax.ShapeDtypeStruct((KC, B, B), F32),
        ),
        in_specs=[smem, any_spec, vmem, vmem, any_spec],
        out_specs=(any_spec, vmem, vmem, vmem),
        scratch_shapes=[
            pltpu.VMEM((KR * B * KC, B), F32),
            pltpu.VMEM((4, 4, B, B), F32),
            pltpu.VMEM((NC, PART, B), F32),
            pltpu.VMEM((NC, PART, B), F32),
            pltpu.VMEM((NZ, PART, B), F32),
            pltpu.VMEM((NY, PART, B), F32),
            pltpu.VMEM((NC, PART, B), F32),
            pltpu.VMEM((NC, XROWS, B), F32),
            pltpu.VMEM((NC, XROWS, B), F32),
            pltpu.VMEM((NC, XROWS, B), F32),
            pltpu.VMEM((NY, NZ, PANEL, B), F32),
            pltpu.VMEM((KR, B, B), F32),
            pltpu.VMEM((KC * B, 6 * B), BF16),
            pltpu.VMEM((KR * B, 6 * B), BF16),
            pltpu.VMEM((KC, 8, B), F32),
            pltpu.VMEM((KR * KC, B, B), F32),
            pltpu.VMEM((B, 2 * B), F32),
            pltpu.VMEM((B, B), F32),
            pltpu.SemaphoreType.DMA((3,)),
            pltpu.SemaphoreType.DMA((88,)),
            pltpu.SemaphoreType.DMA((88,)),
        ],
        compiler_params=pltpu.CompilerParams(
            collective_id=0, has_side_effects=True, vmem_limit_bytes=VMEM_LIMIT
        ),
        name="gather_panel",
    )(
        step_index,
        features.reshape(4, 4, B, B),
        lengthscales.reshape(1, B),
        noise_var,
        component.reshape(KR * B * KC, B),
    )
    pf, trailing = pl.pallas_call(
        update_kernel,
        grid=(KR,),
        out_shape=(
            jax.ShapeDtypeStruct((KR, PART, B), F32),
            jax.ShapeDtypeStruct((KR * B * KC, B), F32),
        ),
        in_specs=[
            smem,
            vmem,
            vmem,
            vmem,
            pl.BlockSpec((KC, B, B), lambda k: (k, 0, 0)),
        ],
        out_specs=(
            vmem,
            pl.BlockSpec((B * KC, B), lambda k: (k, 0)),
        ),
        scratch_shapes=[
            pltpu.VMEM((KR * B, 3 * B), BF16),
            pltpu.VMEM((KC * B, 3 * B), BF16),
        ],
        compiler_params=pltpu.CompilerParams(vmem_limit_bytes=VMEM_LIMIT),
        name="update_blocks",
    )(step_index, linv, rowc, colc, covar)
    return jnp.swapaxes(pf, 1, 2), trailing.reshape(KR, B, KC, B)


def solution(mesh):
    in_specs = (P(None, "col", None), P(), P(None, "col"), P(None, "row", None, "col"), P())
    out_specs = (P(None, "row", "col"), P(None, "row", None, "col"))
    return jax.shard_map(body, mesh=mesh, in_specs=in_specs, out_specs=out_specs, check_vma=False)
```

```python
import functools

import jax
import jax.numpy as jnp
from jax import lax
from jax.experimental import pallas as pl
from jax.experimental.pallas import tpu as pltpu
from jax.sharding import PartitionSpec as P

MESH = pl.DeviceIdType.MESH
F32 = jnp.float32
BF16 = jnp.bfloat16
B = 128
KR, KC, NR, NC = 4, 16, 32, 8
NY, NZ = 4, 8
PART = B // NC
PANEL = KR * PART
FROWS = PART + 8
DEPTH = 5 * B
GATHER_VMEM = 40 * 1024 * 1024
UPDATE_VMEM = 16 * 1024 * 1024


def split2(x):
    high = x.astype(BF16)
    return high, (x - high.astype(F32)).astype(BF16)


def split3(x):
    high = x.astype(BF16)
    rest = x - high.astype(F32)
    mid = rest.astype(BF16)
    low = (rest - mid.astype(F32)).astype(BF16)
    return high, mid, low


def left4(x):
    h, m = split2(x)
    return jnp.concatenate([h, h, m, m], axis=1)


def right4(x):
    h, m = split2(x)
    return jnp.concatenate([h, m, h, m], axis=1)


def left6(x, axis=1):
    h, m, l = split3(x)
    return jnp.concatenate([h, h, m, h, m, l], axis=axis)


def right6(x, axis=1):
    h, m, l = split3(x)
    return jnp.concatenate([h, m, h, l, m, h], axis=axis)


def dot_nt(a, b):
    return lax.dot_general(a, b, (((1,), (1,)), ((), ())), preferred_element_type=F32)


def operand(points, is_left):
    h, m = split2(points)
    rounded = h.astype(F32) + m.astype(F32)
    half = -0.5 * jnp.sum(rounded * rounded, axis=1, keepdims=True)
    pieces = [jnp.broadcast_to(v.astype(F32), points.shape) for v in split3(half)]
    lane = lax.broadcasted_iota(jnp.int32, points.shape, 1)
    first = 3 if is_left else 0
    extra = jnp.where(lane < 6, 1.0, 0.0)
    for i, piece in enumerate(pieces):
        extra = jnp.where(lane == first + i, piece, extra)
    extra = extra.astype(BF16)
    if is_left:
        return jnp.concatenate([h, h, m, m, extra], axis=1)
    return jnp.concatenate([h, m, h, m, extra], axis=1)


def factor_inverse(w_ref, dv_ref):
    size = 16
    lane = lax.broadcasted_iota(jnp.int32, (size, B), 1)
    row = lax.broadcasted_iota(jnp.int32, (size, B), 0)

    def block(b, carry):
        start = pl.multiple_of(b * size, size)
        rows = pl.ds(start, size)
        left = w_ref[rows, 0:B]
        right = w_ref[rows, B : 2 * B]
        rolled = pltpu.roll(left, lax.rem(B - start, B), axis=1)
        cols = [jnp.broadcast_to(rolled[:, k : k + 1], (size, B)) for k in range(size)]
        inv = jnp.zeros((size, B), F32)
        for k in range(size):
            pivot = jnp.broadcast_to(cols[k][k : k + 1, :], (size, B))
            rinv = 1.0 / pivot
            inv = jnp.where(row == k, rinv, inv)
            mult = jnp.where(row > k, cols[k] * rinv, 0.0)
            for j in range(k + 1, size):
                cols[j] = cols[j] - mult * cols[j][k : k + 1, :]
            left = left - mult * left[k : k + 1, :]
            right = right - mult * right[k : k + 1, :]
        w_ref[rows, 0:B] = left
        w_ref[rows, B : 2 * B] = right
        dv_ref[rows, :] = inv
        scaled = jnp.where(lane >= start + size, left * inv, 0.0)
        update = lax.dot_general(
            left6(scaled, 0),
            right6(jnp.concatenate([left, right], axis=1), 0),
            (((0,), (0,)), ((), ())),
            preferred_element_type=F32,
        )
        w_ref[...] = w_ref[...] - update
        return carry

    lax.fori_loop(0, B // size, block, 0)
    return w_ref[:, B : 2 * B] * jnp.sqrt(dv_ref[...])


def gather_kernel(
    step_ref,
    feat_ref,
    ls_hbm,
    noise_hbm,
    comp_ref,
    covar_ref,
    mrow_ref,
    colc_ref,
    pf_ref,
    ls_ref,
    noise_ref,
    comp_v,
    feat_v,
    s_b,
    r_b,
    g_b,
    s_f,
    r_f,
    g_f,
    z_a,
    y_a,
    diag,
    colall,
    rowfeat,
    colcat,
    rowcat,
    rowc,
    w_v,
    dv_v,
    local_sem,
    send_sem,
    recv_sem,
):
    r = lax.axis_index("row")
    c = lax.axis_index("col")
    z = lax.rem(r, NZ)
    y = lax.div(r, NZ)
    axes = {
        "x": (c, NC, lambda i: (r, i)),
        "z": (z, NZ, lambda i: (y * NZ + i, c)),
        "y": (y, NY, lambda i: (i * NZ + z, c)),
    }
    partner = (y * NZ + c, z)
    far = {8: (4, 3, 5, 2, 6, 1, 7), 4: (2, 1, 3)}
    near = {8: (1, 7, 2, 6, 3, 5, 4), 4: (1, 3, 2)}

    def other(me, d, n):
        return lax.rem(me + d, n)

    feat_copy = pltpu.make_async_copy(feat_ref, feat_v, local_sem.at[0])
    comp_copy = pltpu.make_async_copy(comp_ref, comp_v, local_sem.at[1])
    ls_copy = pltpu.make_async_copy(ls_hbm, ls_ref, local_sem.at[2])
    noise_copy = pltpu.make_async_copy(noise_hbm, noise_ref, local_sem.at[3])
    comp_copy.start()
    feat_copy.start()
    ls_copy.start()
    noise_copy.start()

    barrier = pltpu.get_barrier_semaphore()
    for me, n, dev in axes.values():
        for d in far[n]:
            pl.semaphore_signal(barrier, inc=1, device_id=dev(other(me, d, n)), device_id_type=MESH)

    @pl.when(z != c)
    def _():
        pl.semaphore_signal(barrier, inc=1, device_id=partner, device_id_type=MESH)

    def remote(src, dst, send, recv, dev):
        return pltpu.make_async_remote_copy(
            src_ref=src,
            dst_ref=dst,
            send_sem=send_sem.at[send],
            recv_sem=recv_sem.at[recv],
            device_id=dev,
            device_id_type=MESH,
        )

    waits = []

    def spread(axis, src, dst, off, order=far):
        me, n, dev = axes[axis]
        for d in order[n]:
            peer = other(me, d, n)
            copy = remote(src(peer), dst(me), off + d, off + me, dev(peer))
            copy.start()
            waits.append(copy)

    def arrived(axis, dst, off, steps=None):
        me, n, dev = axes[axis]
        for d in steps or near[n]:
            peer = other(me, d, n)
            remote(dst(peer), dst(peer), off + d, off + peer, dev(peer)).wait_recv()

    p = step_ref[0]
    panel_m = lax.div(p, NC)
    panel_c = lax.rem(p, NC)
    panel_k = lax.div(p, NR)
    panel_r = lax.rem(p, NR)
    panel_z = lax.rem(panel_r, NZ)
    panel_y = lax.div(panel_r, NZ)
    comp_copy.wait()
    for k in range(KR):
        block = comp_v[pl.ds(k * (B * KC) + panel_m, B, stride=KC), :]
        s_b[:, k] = block.reshape(NC, PART, B)
    feat_copy.wait()
    ls_copy.wait()
    noise_copy.wait()
    inv_ls = 1.0 / ls_ref[...]
    feat_p = feat_v[lax.div(panel_m, 4), lax.rem(panel_m, 4)] * inv_ls
    s_f[:, 0:PART, :] = feat_p.reshape(NC, PART, B)
    noise_p = noise_ref[pl.ds(panel_m, 1), :]
    s_f[:, PART:FROWS, :] = jnp.broadcast_to(noise_p.reshape(1, 1, B), (NC, 8, B))
    r_b[c] = s_b[c]
    r_f[c] = s_f[c]

    @pl.when(z != c)
    def _():
        pl.semaphore_wait(barrier, 2 * NC + NY - 2)

    @pl.when(z == c)
    def _():
        pl.semaphore_wait(barrier, 2 * NC + NY - 3)

    spread("x", lambda i: s_b.at[i], lambda i: r_b.at[i], 0)
    spread("x", lambda i: s_f.at[i], lambda i: r_f.at[i], 8)

    feat_move = [remote(feat_v.at[k, y], rowfeat.at[k], 124 + k, 124 + k, partner) for k in range(KR)]

    @pl.when(z != c)
    def _():
        for copy in feat_move:
            copy.start()

    @pl.when(z == c)
    def _():
        for k in range(KR):
            rowfeat[k] = feat_v[k, y]

    def prepare(m, carry):
        pts = feat_v[lax.div(m, 4), lax.rem(m, 4)] * inv_ls
        colcat[pl.ds(pl.multiple_of(m * B, B), B), :] = operand(pts, False)
        return carry

    lax.fori_loop(0, KC, prepare, 0, unroll=4)

    arrived("x", lambda i: r_b.at[i], 0)
    g_b[c] = r_b[panel_c]
    move = remote(g_b.at[c], colall.at[y, c], 16, 16, partner)
    moved = remote(g_b.at[c], colall.at[y, z], 16, 16, partner)

    @pl.when(z != c)
    def _():
        move.start()

    @pl.when(z == c)
    def _():
        colall[y, z] = g_b[c]

    z_a[z] = r_b[panel_c, panel_k]
    spread("z", lambda i: z_a.at[z], lambda i: z_a.at[i], 20)
    spread("x", lambda i: g_b.at[c], lambda i: g_b.at[i], 28)
    arrived("x", lambda i: r_f.at[i], 8)
    g_f[c] = r_f[panel_c]
    spread("x", lambda i: g_f.at[c], lambda i: g_f.at[i], 36)

    @pl.when(z != c)
    def _():
        for copy in feat_move:
            copy.wait_recv()

    for k in range(KR):
        rowcat[k * B : (k + 1) * B, :] = operand(rowfeat[k] * inv_ls, True)
    eye = lax.broadcasted_iota(jnp.int32, (B, B), 0) == lax.broadcasted_iota(jnp.int32, (B, B), 1)

    def cover(part):
        for m2 in (2 * part, 2 * part + 1):
            expo = dot_nt(rowcat[...], colcat[m2 * 2 * B : (m2 + 1) * 2 * B, :])
            for j in range(2):
                m = m2 * 2 + j
                for k in range(KR):
                    value = jnp.exp(expo[k * B : (k + 1) * B, j * B : (j + 1) * B])
                    value = value + comp_v[pl.ds(k * (B * KC) + m, B, stride=KC), :]
                    if m // 4 == k:
                        same = jnp.logical_and(z == c, y == m % 4)
                        value = value + jnp.where(jnp.logical_and(eye, same), noise_ref[m : m + 1, :], 0.0)
                    covar_ref[m, k * B : (k + 1) * B, :] = value

    def forward(piece, slot):
        for d in near[NY]:
            peer = other(y, d, NY)
            copy = remote(
                colall.at[y, piece],
                colall.at[y, piece],
                60 + slot * 4 + d,
                92 + y * NZ + piece,
                axes["y"][2](peer),
            )
            copy.start()
            waits.append(copy)

    def relay(steps):
        for d in steps:
            arrived("z", lambda i: colall.at[y, i], 52, (d,))
            forward(other(z, d, NZ), d)

    arrived("z", lambda i: z_a.at[i], 20)
    y_a[y] = z_a[panel_z]
    spread("y", lambda i: y_a.at[y], lambda i: y_a.at[i], 44)

    @pl.when(z != c)
    def _():
        moved.wait_recv()

    spread("z", lambda i: colall.at[y, z], lambda i: colall.at[y, i], 52, near)
    forward(z, 0)
    cover(0)
    arrived("y", lambda i: y_a.at[i], 44)
    diag[c] = y_a[panel_y]
    spread("x", lambda i: diag.at[c], lambda i: diag.at[i], 128)
    relay((1, 7))
    cover(1)
    relay((2, 6))
    cover(2)
    relay((3, 5, 4))
    cover(3)

    arrived("x", lambda i: g_b.at[i], 28)
    arrived("x", lambda i: g_f.at[i], 36)
    pts_p = g_f[:, 0:PART, :].reshape(B, B)
    left_p, right_p = operand(pts_p, True), operand(pts_p, False)
    noise_p = jnp.where(eye, g_f[0, PART : PART + 1, :], 0.0)
    kernel_p = jnp.exp(dot_nt(left_p, right_p)) + noise_p
    kernel_row = jnp.exp(dot_nt(rowcat[...], right_p))
    for k in range(KR):
        here = k * NR + r == p
        raw = g_b[:, k].reshape(B, B)
        rowc[k * B : (k + 1) * B, :] = kernel_row[k * B : (k + 1) * B, :] + raw + jnp.where(here, noise_p, 0.0)

    arrived("x", lambda i: diag.at[i], 128)
    w_v[:, 0:B] = kernel_p + diag[...].reshape(B, B)
    w_v[:, B : 2 * B] = jnp.where(eye, 1.0, 0.0)
    linv = factor_inverse(w_v, dv_v)
    dv_v[...] = linv
    solved = dot_nt(left6(rowc[...]), right6(linv))
    weights = jnp.dot(left6(solved), right6(linv, 0), preferred_element_type=F32)
    share = right6(dv_v[pl.ds(pl.multiple_of(c * PART, PART), PART), :])
    mine = dot_nt(share, left6(rowc[...]))
    row = lax.broadcasted_iota(jnp.int32, (PART, B), 1)
    col = lax.broadcasted_iota(jnp.int32, (PART, B), 0) + c * PART
    for k in range(KR):
        w = k * NR + r
        mrow_ref[k * B : (k + 1) * B, :] = jnp.where(w > p, weights[k * B : (k + 1) * B, :], 0.0)
        keep = jnp.logical_or(w > p, jnp.logical_and(w == p, col <= row))
        pf_ref[k] = jnp.where(keep, mine[:, k * B : (k + 1) * B], 0.0)
    for m in range(KC):
        kern = jnp.exp(dot_nt(colcat[m * B : (m + 1) * B, :], left_p))
        colc_ref[m * B : (m + 1) * B, :] = kern

    for d in near[NY]:
        peer = other(y, d, NY)
        for piece in range(NZ):
            landed = colall.at[peer, piece]
            remote(landed, landed, 60, 92 + peer * NZ + piece, axes["y"][2](peer)).wait_recv()
    for m in range(KC):
        k, q = m // NY, m % NY
        raw = colall[q, :, k].reshape(B, B)
        rows = slice(m * B, (m + 1) * B)
        colc_ref[rows, :] = jnp.where(m * NC + c > p, colc_ref[rows, :] + raw, 0.0)

    for copy in waits:
        copy.wait_send()

    @pl.when(z != c)
    def _():
        move.wait_send()
        for copy in feat_move:
            copy.wait_send()


def update_kernel(covar_ref, mrow_ref, colc_ref, pf_in, out_ref, pf_ref, out_v, sem):
    left = left4(mrow_ref[...])
    copies = []
    for half in range(2):
        for pair in range(2):
            rows = slice(pair * 2 * B, (pair + 1) * 2 * B)
            for m2 in range(half * 4, half * 4 + 4):
                update = dot_nt(left[rows, :], right4(colc_ref[m2 * 2 * B : (m2 + 1) * 2 * B, :]))
                for j in range(2):
                    m = m2 * 2 + j
                    value = covar_ref[m, rows, :] - update[:, j * B : (j + 1) * B]
                    out_v[pl.ds(pair * 2 * B * KC + m, 2 * B, stride=KC), :] = value
            view = out_v.reshape(KR * B, KC, B)
            part = (pl.ds(pair * 2 * B, 2 * B), pl.ds(half * 8, 8))
            copy = pltpu.make_async_copy(view.at[part], out_ref.at[part], sem.at[half * 2 + pair])
            copy.start()
            copies.append(copy)
    pf_ref[...] = pf_in[...]
    for copy in copies:
        copy.wait()


def in_hbm(x):
    return pltpu.with_memory_space_constraint(x, pltpu.HBM)


def body(features, lengthscales, noise_var, component, step_index):
    hbm = pl.BlockSpec(memory_space=pltpu.HBM)
    vmem = pl.BlockSpec(memory_space=pltpu.VMEM)
    smem = pl.BlockSpec(memory_space=pltpu.SMEM)
    covar, mrow, colc, pf = pl.pallas_call(
        gather_kernel,
        out_shape=(
            jax.ShapeDtypeStruct((KC, KR * B, B), F32),
            jax.ShapeDtypeStruct((KR * B, B), F32),
            jax.ShapeDtypeStruct((KC * B, B), F32),
            jax.ShapeDtypeStruct((KR, PART, B), F32),
        ),
        in_specs=[smem, hbm, hbm, hbm, hbm],
        out_specs=(vmem, vmem, vmem, vmem),
        scratch_shapes=[
            pltpu.VMEM((1, B), F32),
            pltpu.VMEM((KC, B), F32),
            pltpu.VMEM((KR * B * KC, B), F32),
            pltpu.VMEM((4, 4, B, B), F32),
            pltpu.VMEM((NC, KR, PART, B), F32),
            pltpu.VMEM((NC, KR, PART, B), F32),
            pltpu.VMEM((NC, KR, PART, B), F32),
            pltpu.VMEM((NC, FROWS, B), F32),
            pltpu.VMEM((NC, FROWS, B), F32),
            pltpu.VMEM((NC, FROWS, B), F32),
            pltpu.VMEM((NZ, PART, B), F32),
            pltpu.VMEM((NY, PART, B), F32),
            pltpu.VMEM((NC, PART, B), F32),
            pltpu.VMEM((NY, NZ, KR, PART, B), F32),
            pltpu.VMEM((KR, B, B), F32),
            pltpu.VMEM((KC * B, DEPTH), BF16),
            pltpu.VMEM((KR * B, DEPTH), BF16),
            pltpu.VMEM((KR * B, B), F32),
            pltpu.VMEM((B, 2 * B), F32),
            pltpu.VMEM((B, B), F32),
            pltpu.SemaphoreType.DMA((4,)),
            pltpu.SemaphoreType.DMA((136,)),
            pltpu.SemaphoreType.DMA((136,)),
        ],
        compiler_params=pltpu.CompilerParams(
            collective_id=0, has_side_effects=True, vmem_limit_bytes=GATHER_VMEM
        ),
        name="gather_panel",
    )(
        step_index,
        in_hbm(features.reshape(4, 4, B, B)),
        in_hbm(lengthscales.reshape(1, B)),
        in_hbm(noise_var),
        in_hbm(component.reshape(KR * B * KC, B)),
    )
    trailing, pf = pl.pallas_call(
        update_kernel,
        out_shape=(
            jax.ShapeDtypeStruct((KR * B, KC, B), F32),
            jax.ShapeDtypeStruct((KR, PART, B), F32),
        ),
        in_specs=[vmem, vmem, vmem, vmem],
        out_specs=(hbm, vmem),
        scratch_shapes=[
            pltpu.VMEM((KR * B * KC, B), F32),
            pltpu.SemaphoreType.DMA((4,)),
        ],
        compiler_params=pltpu.CompilerParams(vmem_limit_bytes=UPDATE_VMEM),
        name="update_blocks",
    )(covar, mrow, colc, pf)
    return jnp.swapaxes(pf, 1, 2), trailing.reshape(KR, B, KC, B)


def solution(mesh):
    in_specs = (P(None, "col", None), P(), P(None, "col"), P(None, "row", None, "col"), P())
    out_specs = (P(None, "row", "col"), P(None, "row", None, "col"))
    return jax.shard_map(body, mesh=mesh, in_specs=in_specs, out_specs=out_specs, check_vma=False)
```

```python
import functools

import jax
import jax.numpy as jnp
from jax import lax
from jax.experimental import pallas as pl
from jax.experimental.pallas import tpu as pltpu
from jax.sharding import PartitionSpec as P

MESH = pl.DeviceIdType.MESH
F32 = jnp.float32
BF16 = jnp.bfloat16
B = 128
KR, KC, NR, NC = 4, 16, 32, 8
NY, NZ = 4, 8
PART = B // NC
GROUP = 2 * KR + 2
DEPTH = 5 * B
GATHER_VMEM = 40 * 1024 * 1024
UPDATE_VMEM = 16 * 1024 * 1024


def split2(x):
    high = x.astype(BF16)
    return high, (x - high.astype(F32)).astype(BF16)


def split3(x):
    high = x.astype(BF16)
    rest = x - high.astype(F32)
    mid = rest.astype(BF16)
    low = (rest - mid.astype(F32)).astype(BF16)
    return high, mid, low


def left4(x):
    h, m = split2(x)
    return jnp.concatenate([h, h, m, m], axis=1)


def right4(x):
    h, m = split2(x)
    return jnp.concatenate([h, m, h, m], axis=1)


def left6(x, axis=1):
    h, m, l = split3(x)
    return jnp.concatenate([h, h, m, h, m, l], axis=axis)


def right6(x, axis=1):
    h, m, l = split3(x)
    return jnp.concatenate([h, m, h, l, m, h], axis=axis)


def dot_nt(a, b):
    return lax.dot_general(a, b, (((1,), (1,)), ((), ())), preferred_element_type=F32)


def operand(points, is_left):
    h, m = split2(points)
    rounded = h.astype(F32) + m.astype(F32)
    half = -0.5 * jnp.sum(rounded * rounded, axis=1, keepdims=True)
    pieces = [jnp.broadcast_to(v.astype(F32), points.shape) for v in split3(half)]
    lane = lax.broadcasted_iota(jnp.int32, points.shape, 1)
    first = 3 if is_left else 0
    extra = jnp.where(lane < 6, 1.0, 0.0)
    for i, piece in enumerate(pieces):
        extra = jnp.where(lane == first + i, piece, extra)
    extra = extra.astype(BF16)
    if is_left:
        return jnp.concatenate([h, h, m, m, extra], axis=1)
    return jnp.concatenate([h, m, h, m, extra], axis=1)


def factor_inverse(w_ref, dv_ref):
    size = 16
    lane = lax.broadcasted_iota(jnp.int32, (size, B), 1)
    row = lax.broadcasted_iota(jnp.int32, (size, B), 0)

    def block(b, carry):
        start = pl.multiple_of(b * size, size)
        rows = pl.ds(start, size)
        left = w_ref[rows, 0:B]
        right = w_ref[rows, B : 2 * B]
        rolled = pltpu.roll(left, lax.rem(B - start, B), axis=1)
        cols = [jnp.broadcast_to(rolled[:, k : k + 1], (size, B)) for k in range(size)]
        inv = jnp.zeros((size, B), F32)
        for k in range(size):
            pivot = jnp.broadcast_to(cols[k][k : k + 1, :], (size, B))
            rinv = 1.0 / pivot
            inv = jnp.where(row == k, rinv, inv)
            mult = jnp.where(row > k, cols[k] * rinv, 0.0)
            for j in range(k + 1, size):
                cols[j] = cols[j] - mult * cols[j][k : k + 1, :]
            left = left - mult * left[k : k + 1, :]
            right = right - mult * right[k : k + 1, :]
        w_ref[rows, 0:B] = left
        w_ref[rows, B : 2 * B] = right
        dv_ref[rows, :] = inv
        scaled = jnp.where(lane >= start + size, left * inv, 0.0)
        update = lax.dot_general(
            left6(scaled, 0),
            right6(jnp.concatenate([left, right], axis=1), 0),
            (((0,), (0,)), ((), ())),
            preferred_element_type=F32,
        )
        w_ref[...] = w_ref[...] - update
        return carry

    lax.fori_loop(0, B // size, block, 0)
    return w_ref[:, B : 2 * B] * jnp.sqrt(dv_ref[...])


def gather_kernel(
    step_ref,
    feat_ref,
    ls_hbm,
    noise_hbm,
    comp_ref,
    covar_ref,
    mrow_ref,
    colc_ref,
    pf_ref,
    ls_ref,
    noise_ref,
    comp_0,
    comp_1,
    comp_2,
    comp_3,
    feat_v,
    s_a,
    r_a,
    s_b,
    r_b,
    s_f,
    r_f,
    group,
    z_a,
    y_a,
    diag,
    ybuf,
    xbuf,
    colcat,
    rowcat,
    rowc,
    w_v,
    dv_v,
    local_sem,
    send_sem,
    recv_sem,
):
    r = lax.axis_index("row")
    c = lax.axis_index("col")
    z = lax.rem(r, NZ)
    y = lax.div(r, NZ)
    axes = {
        "x": (c, NC, lambda i: (r, i)),
        "z": (z, NZ, lambda i: (y * NZ + i, c)),
        "y": (y, NY, lambda i: (i * NZ + z, c)),
    }
    partner = (y * NZ + c, z)
    sibling = c + 1 - 2 * lax.rem(c, 2)
    far = {8: (4, 3, 5, 2, 6, 1, 7), 4: (2, 1, 3)}
    near = {8: (1, 7, 2, 6, 3, 5, 4), 4: (1, 3, 2)}

    def other(me, d, n):
        return lax.rem(me + d, n)

    comp_v = (comp_0, comp_1, comp_2, comp_3)
    comp_copies = [
        pltpu.make_async_copy(comp_ref.at[pl.ds(k * B * KC, B * KC)], comp_v[k], local_sem.at[4 + k])
        for k in range(KR)
    ]
    feat_copy = pltpu.make_async_copy(feat_ref, feat_v, local_sem.at[0])
    ls_copy = pltpu.make_async_copy(ls_hbm, ls_ref, local_sem.at[1])
    noise_copy = pltpu.make_async_copy(noise_hbm, noise_ref, local_sem.at[2])
    for copy in comp_copies:
        copy.start()
    feat_copy.start()
    ls_copy.start()
    noise_copy.start()

    barrier = pltpu.get_barrier_semaphore()
    for me, n, dev in axes.values():
        for d in far[n]:
            pl.semaphore_signal(barrier, inc=1, device_id=dev(other(me, d, n)), device_id_type=MESH)

    @pl.when(z != c)
    def _():
        pl.semaphore_signal(barrier, inc=1, device_id=partner, device_id_type=MESH)

    def remote(src, dst, send, recv, dev):
        return pltpu.make_async_remote_copy(
            src_ref=src,
            dst_ref=dst,
            send_sem=send_sem.at[send],
            recv_sem=recv_sem.at[recv],
            device_id=dev,
            device_id_type=MESH,
        )

    waits = []

    def post(copy):
        copy.start()
        waits.append(copy)

    def spread(axis, src, dst, off, order=far):
        me, n, dev = axes[axis]
        for d in order[n]:
            peer = other(me, d, n)
            post(remote(src(peer), dst(me), off + d, off + me, dev(peer)))

    def arrived(axis, dst, off, steps=None):
        me, n, dev = axes[axis]
        for d in steps or near[n]:
            peer = other(me, d, n)
            remote(dst(peer), dst(peer), off + d, off + peer, dev(peer)).wait_recv()

    p = step_ref[0]
    panel_m = lax.div(p, NC)
    panel_c = lax.rem(p, NC)
    panel_k = lax.div(p, NR)
    panel_r = lax.rem(p, NR)
    panel_z = lax.rem(panel_r, NZ)
    panel_y = lax.div(panel_r, NZ)

    for k in range(KR):
        comp_copies[k].wait()
        block = comp_v[k][pl.ds(panel_m, B, stride=KC), :]
        s_b[:, k] = block.reshape(NC, PART, B)
    s_a[...] = s_b[:, panel_k]
    r_a[c] = s_a[c]
    r_b[c] = s_b[c]

    @pl.when(z != c)
    def _():
        pl.semaphore_wait(barrier, 2 * NC + NY - 2)

    @pl.when(z == c)
    def _():
        pl.semaphore_wait(barrier, 2 * NC + NY - 3)

    spread("x", lambda i: s_a.at[i], lambda i: r_a.at[i], 0)
    spread("x", lambda i: s_b.at[i], lambda i: r_b.at[i], 8)
    feat_copy.wait()
    ls_copy.wait()
    noise_copy.wait()

    part = pl.ds(pl.multiple_of(z * PART, PART), PART)
    feat_out = remote(feat_v.at[:, y, part, :], group.at[z, 6:10], 24, 24, partner)
    feat_in = remote(feat_v.at[:, y, part, :], group.at[c, 6:10], 24, 24, partner)

    @pl.when(z != c)
    def _():
        feat_out.start()

    @pl.when(z == c)
    def _():
        for k in range(KR):
            group[c, 6 + k] = feat_v[k, y, part, :]

    inv_ls = 1.0 / ls_ref[...]
    feat_p = feat_v[lax.div(panel_m, 4), lax.rem(panel_m, 4)] * inv_ls
    s_f[:, 0] = feat_p.reshape(NC, PART, B)
    noise_p = noise_ref[pl.ds(panel_m, 1), :]
    s_f[:, 1] = jnp.broadcast_to(noise_p.reshape(1, 1, B), (NC, PART, B))
    r_f[c] = s_f[c]
    spread("x", lambda i: s_f.at[i], lambda i: r_f.at[i], 16)

    def prepare(m, carry):
        pts = feat_v[lax.div(m, 4), lax.rem(m, 4)] * inv_ls
        colcat[pl.ds(pl.multiple_of(m * B, B), B), :] = operand(pts, False)
        return carry

    lax.fori_loop(0, KC // 2, prepare, 0, unroll=4)

    arrived("x", lambda i: r_a.at[i], 0)
    z_a[z] = r_a[panel_c]
    spread("z", lambda i: z_a.at[z], lambda i: z_a.at[i], 32)

    def over_y(rel):
        for d in near[NY]:
            peer = other(y, d, NY)
            slot = NY - d
            send = remote(
                ybuf.at[rel, 0], ybuf.at[rel, slot], 64 + rel * 4 + d, 64 + rel * 4 + slot, axes["y"][2](peer)
            )
            post(send)

    def from_y(rel):
        for d in near[NY]:
            peer = other(y, d, NY)
            here = ybuf.at[rel, d]
            remote(here, here, 64, 64 + rel * 4 + d, axes["y"][2](peer)).wait_recv()

    over_x_waits = []

    def over_x(rel, first, count, off):
        target = other(z, rel, NZ)
        src = ybuf.at[rel, first : first + count]
        dst = xbuf.at[c, first : first + count]
        send = remote(src, dst, off + rel, off + c, (r, target))
        here = pltpu.make_async_copy(src, dst, send_sem.at[off + rel])

        @pl.when(target != c)
        def _():
            send.start()

        @pl.when(target == c)
        def _():
            here.start()

        over_x_waits.append((target, send, here))

    arrived("x", lambda i: r_b.at[i], 8)
    ybuf[0, 0] = r_b[panel_c]
    group[c, 0:4] = r_b[panel_c]
    for d in near[NZ]:
        peer = other(z, d, NZ)
        post(remote(ybuf.at[0, 0], ybuf.at[NZ - d, 0], 40 + d, 40 + NZ - d, axes["z"][2](peer)))
    over_y(0)
    over_x(0, 0, 1, 96)

    def relay(steps):
        for d in steps:
            here = ybuf.at[d, 0]
            remote(here, here, 40, 40 + d, axes["z"][2](other(z, d, NZ))).wait_recv()
            over_y(d)
            over_x(d, 0, 1, 96)

    lax.fori_loop(KC // 2, KC, prepare, 0, unroll=4)
    relay((1, 7))

    arrived("x", lambda i: r_f.at[i], 16)
    group[c, 4:6] = r_f[panel_c]

    @pl.when(z != c)
    def _():
        feat_in.wait_recv()

    mates = [(0, sibling)] + [(d, other(c, d, NC)) for d in (2, 6, 4)]
    for d, peer in mates[1:] + mates[:1]:
        post(remote(group.at[c], group.at[c], 112 + d, 112 + c, (r, peer)))

    arrived("z", lambda i: z_a.at[i], 32)
    y_a[y] = z_a[panel_z]
    spread("y", lambda i: y_a.at[y], lambda i: y_a.at[i], 48)
    relay((2, 6))
    from_y(0)
    over_x(0, 1, 3, 104)

    for d, peer in mates[1:]:
        slot = group.at[peer]
        remote(slot, slot, 112 + d, 112 + peer, (r, peer)).wait_recv()
        post(remote(slot, slot, 113 + d, 112 + peer, (r, sibling)))

    arrived("y", lambda i: y_a.at[i], 48)
    diag[c] = y_a[panel_y]
    spread("x", lambda i: diag.at[c], lambda i: diag.at[i], 56)
    relay((3, 5))
    for d in (1, 7):
        from_y(d)
        over_x(d, 1, 3, 104)
    for d in (0, 2, 6, 4):
        slot = group.at[other(sibling, d, NC)]
        remote(slot, slot, 112, 112 + other(sibling, d, NC), (r, sibling)).wait_recv()

    for k in range(KR):
        rows = group[:, 6 + k].reshape(B, B)
        rowcat[k * B : (k + 1) * B, :] = operand(rows * inv_ls, True)
    eye = lax.broadcasted_iota(jnp.int32, (B, B), 0) == lax.broadcasted_iota(jnp.int32, (B, B), 1)

    def cover(quarter):
        for m2 in (2 * quarter, 2 * quarter + 1):
            expo = dot_nt(rowcat[...], colcat[m2 * 2 * B : (m2 + 1) * 2 * B, :])
            for j in range(2):
                m = m2 * 2 + j
                for k in range(KR):
                    value = jnp.exp(expo[k * B : (k + 1) * B, j * B : (j + 1) * B])
                    value = value + comp_v[k][pl.ds(m, B, stride=KC), :]
                    if m // 4 == k:
                        same = jnp.logical_and(z == c, y == m % 4)
                        value = value + jnp.where(jnp.logical_and(eye, same), noise_ref[m : m + 1, :], 0.0)
                    covar_ref[m, k * B : (k + 1) * B, :] = value

    cover(0)
    relay((4,))
    for d in (2, 6):
        from_y(d)
        over_x(d, 1, 3, 104)
    cover(1)
    for d in (3, 5):
        from_y(d)
        over_x(d, 1, 3, 104)
    cover(2)
    from_y(4)
    over_x(4, 1, 3, 104)
    cover(3)

    pts_p = group[:, 4].reshape(B, B)
    left_p, right_p = operand(pts_p, True), operand(pts_p, False)
    noise_p = jnp.where(eye, group[0, 5, 0:1, :], 0.0)
    kernel_p = jnp.exp(dot_nt(left_p, right_p)) + noise_p
    kernel_row = jnp.exp(dot_nt(rowcat[...], right_p))
    for k in range(KR):
        here = k * NR + r == p
        raw = group[:, k].reshape(B, B)
        rowc[k * B : (k + 1) * B, :] = kernel_row[k * B : (k + 1) * B, :] + raw + jnp.where(here, noise_p, 0.0)

    arrived("x", lambda i: diag.at[i], 56)
    w_v[:, 0:B] = kernel_p + diag[...].reshape(B, B)
    w_v[:, B : 2 * B] = jnp.where(eye, 1.0, 0.0)
    linv = factor_inverse(w_v, dv_v)
    dv_v[...] = linv
    solved = dot_nt(left6(rowc[...]), right6(linv))
    weights = jnp.dot(left6(solved), right6(linv, 0), preferred_element_type=F32)
    share = right6(dv_v[pl.ds(pl.multiple_of(c * PART, PART), PART), :])
    mine = dot_nt(share, left6(rowc[...]))
    row = lax.broadcasted_iota(jnp.int32, (PART, B), 1)
    col = lax.broadcasted_iota(jnp.int32, (PART, B), 0) + c * PART
    for k in range(KR):
        w = k * NR + r
        mrow_ref[k * B : (k + 1) * B, :] = jnp.where(w > p, weights[k * B : (k + 1) * B, :], 0.0)
        keep = jnp.logical_or(w > p, jnp.logical_and(w == p, col <= row))
        pf_ref[k] = jnp.where(keep, mine[:, k * B : (k + 1) * B], 0.0)

    def column(m, carry):
        rows = pl.ds(pl.multiple_of(m * B, B), B)
        colc_ref[rows, :] = jnp.exp(dot_nt(colcat[rows, :], left_p))
        return carry

    lax.fori_loop(0, KC, column, 0, unroll=8)

    for target, send, here in over_x_waits:

        @pl.when(target != c)
        def _(send=send):
            send.wait_send()

        @pl.when(target == c)
        def _(here=here):
            here.wait()

    for d in near[NC]:
        peer = other(c, d, NC)
        for off, first, count in ((96, 0, 1), (104, 1, 3)):
            here = xbuf.at[peer, first : first + count]
            remote(here, here, off, off + peer, (r, peer)).wait_recv()
    for rel in range(NY):
        for k in range(KR):
            m = k * 4 + other(y, rel, NY)
            raw = xbuf[:, rel, k].reshape(B, B)
            rows = pl.ds(pl.multiple_of(m * B, B), B)
            colc_ref[rows, :] = jnp.where(m * NC + c > p, colc_ref[rows, :] + raw, 0.0)

    for copy in waits:
        copy.wait_send()

    @pl.when(z != c)
    def _():
        feat_out.wait_send()


def update_kernel(covar_ref, mrow_ref, colc_ref, pf_in, out_ref, pf_ref, out_v, sem):
    left = left4(mrow_ref[...])
    copies = []
    for half in range(2):
        for pair in range(2):
            rows = slice(pair * 2 * B, (pair + 1) * 2 * B)
            for m2 in range(half * 4, half * 4 + 4):
                update = dot_nt(left[rows, :], right4(colc_ref[m2 * 2 * B : (m2 + 1) * 2 * B, :]))
                for j in range(2):
                    m = m2 * 2 + j
                    value = covar_ref[m, rows, :] - update[:, j * B : (j + 1) * B]
                    out_v[pl.ds(pair * 2 * B * KC + m, 2 * B, stride=KC), :] = value
            view = out_v.reshape(KR * B, KC, B)
            part = (pl.ds(pair * 2 * B, 2 * B), pl.ds(half * 8, 8))
            copy = pltpu.make_async_copy(view.at[part], out_ref.at[part], sem.at[half * 2 + pair])
            copy.start()
            copies.append(copy)
    pf_ref[...] = pf_in[...]
    for copy in copies:
        copy.wait()


def in_hbm(x):
    return pltpu.with_memory_space_constraint(x, pltpu.HBM)


def body(features, lengthscales, noise_var, component, step_index):
    hbm = pl.BlockSpec(memory_space=pltpu.HBM)
    vmem = pl.BlockSpec(memory_space=pltpu.VMEM)
    smem = pl.BlockSpec(memory_space=pltpu.SMEM)
    covar, mrow, colc, pf = pl.pallas_call(
        gather_kernel,
        out_shape=(
            jax.ShapeDtypeStruct((KC, KR * B, B), F32),
            jax.ShapeDtypeStruct((KR * B, B), F32),
            jax.ShapeDtypeStruct((KC * B, B), F32),
            jax.ShapeDtypeStruct((KR, PART, B), F32),
        ),
        in_specs=[smem, hbm, hbm, hbm, hbm],
        out_specs=(vmem, vmem, vmem, vmem),
        scratch_shapes=[
            pltpu.VMEM((1, B), F32),
            pltpu.VMEM((KC, B), F32),
            pltpu.VMEM((B * KC, B), F32),
            pltpu.VMEM((B * KC, B), F32),
            pltpu.VMEM((B * KC, B), F32),
            pltpu.VMEM((B * KC, B), F32),
            pltpu.VMEM((4, 4, B, B), F32),
            pltpu.VMEM((NC, PART, B), F32),
            pltpu.VMEM((NC, PART, B), F32),
            pltpu.VMEM((NC, KR, PART, B), F32),
            pltpu.VMEM((NC, KR, PART, B), F32),
            pltpu.VMEM((NC, 2, PART, B), F32),
            pltpu.VMEM((NC, 2, PART, B), F32),
            pltpu.VMEM((NC, GROUP, PART, B), F32),
            pltpu.VMEM((NZ, PART, B), F32),
            pltpu.VMEM((NY, PART, B), F32),
            pltpu.VMEM((NC, PART, B), F32),
            pltpu.VMEM((NZ, NY, KR, PART, B), F32),
            pltpu.VMEM((NC, NY, KR, PART, B), F32),
            pltpu.VMEM((KC * B, DEPTH), BF16),
            pltpu.VMEM((KR * B, DEPTH), BF16),
            pltpu.VMEM((KR * B, B), F32),
            pltpu.VMEM((B, 2 * B), F32),
            pltpu.VMEM((B, B), F32),
            pltpu.SemaphoreType.DMA((8,)),
            pltpu.SemaphoreType.DMA((136,)),
            pltpu.SemaphoreType.DMA((136,)),
        ],
        compiler_params=pltpu.CompilerParams(
            collective_id=0, has_side_effects=True, vmem_limit_bytes=GATHER_VMEM
        ),
        name="gather_panel",
    )(
        step_index,
        in_hbm(features.reshape(4, 4, B, B)),
        in_hbm(lengthscales.reshape(1, B)),
        in_hbm(noise_var),
        in_hbm(component.reshape(KR * B * KC, B)),
    )
    trailing, pf = pl.pallas_call(
        update_kernel,
        out_shape=(
            jax.ShapeDtypeStruct((KR * B, KC, B), F32),
            jax.ShapeDtypeStruct((KR, PART, B), F32),
        ),
        in_specs=[vmem, vmem, vmem, vmem],
        out_specs=(hbm, vmem),
        scratch_shapes=[
            pltpu.VMEM((KR * B * KC, B), F32),
            pltpu.SemaphoreType.DMA((4,)),
        ],
        compiler_params=pltpu.CompilerParams(vmem_limit_bytes=UPDATE_VMEM),
        name="update_blocks",
    )(covar, mrow, colc, pf)
    return jnp.swapaxes(pf, 1, 2), trailing.reshape(KR, B, KC, B)


def solution(mesh):
    in_specs = (P(None, "col", None), P(), P(None, "col"), P(None, "row", None, "col"), P())
    out_specs = (P(None, "row", "col"), P(None, "row", None, "col"))
    return jax.shard_map(body, mesh=mesh, in_specs=in_specs, out_specs=out_specs, check_vma=False)
```

```python
import functools

import jax
import jax.numpy as jnp
from jax import lax
from jax.experimental import pallas as pl
from jax.experimental.pallas import tpu as pltpu
from jax.sharding import PartitionSpec as P

MESH = pl.DeviceIdType.MESH
F32 = jnp.float32
BF16 = jnp.bfloat16
B = 128
KR, KC, NR, NC = 4, 16, 32, 8
NY, NZ = 4, 8
PART = B // NC
GROUP = 2 * KR + 2
DEPTH = 5 * B
GATHER_VMEM = 40 * 1024 * 1024
UPDATE_VMEM = 16 * 1024 * 1024


def split2(x):
    high = x.astype(BF16)
    return high, (x - high.astype(F32)).astype(BF16)


def split3(x):
    high = x.astype(BF16)
    rest = x - high.astype(F32)
    mid = rest.astype(BF16)
    low = (rest - mid.astype(F32)).astype(BF16)
    return high, mid, low


def left4(x):
    h, m = split2(x)
    return jnp.concatenate([h, h, m, m], axis=1)


def right4(x):
    h, m = split2(x)
    return jnp.concatenate([h, m, h, m], axis=1)


def left6(x, axis=1):
    h, m, l = split3(x)
    return jnp.concatenate([h, h, m, h, m, l], axis=axis)


def right6(x, axis=1):
    h, m, l = split3(x)
    return jnp.concatenate([h, m, h, l, m, h], axis=axis)


def dot_nt(a, b):
    return lax.dot_general(a, b, (((1,), (1,)), ((), ())), preferred_element_type=F32)


def operand(points, is_left):
    h, m = split2(points)
    rounded = h.astype(F32) + m.astype(F32)
    half = -0.5 * jnp.sum(rounded * rounded, axis=1, keepdims=True)
    pieces = [jnp.broadcast_to(v.astype(F32), points.shape) for v in split3(half)]
    lane = lax.broadcasted_iota(jnp.int32, points.shape, 1)
    first = 3 if is_left else 0
    extra = jnp.where(lane < 6, 1.0, 0.0)
    for i, piece in enumerate(pieces):
        extra = jnp.where(lane == first + i, piece, extra)
    extra = extra.astype(BF16)
    if is_left:
        return jnp.concatenate([h, h, m, m, extra], axis=1)
    return jnp.concatenate([h, m, h, m, extra], axis=1)


def eliminate(w_ref, dv_ref, first, last):
    size = 16
    lane = lax.broadcasted_iota(jnp.int32, (size, B), 1)
    row = lax.broadcasted_iota(jnp.int32, (size, B), 0)

    def block(b, carry):
        start = pl.multiple_of(b * size, size)
        rows = pl.ds(start, size)
        left = w_ref[rows, 0:B]
        right = w_ref[rows, B : 2 * B]
        rolled = pltpu.roll(left, lax.rem(B - start, B), axis=1)
        cols = [jnp.broadcast_to(rolled[:, k : k + 1], (size, B)) for k in range(size)]
        inv = jnp.zeros((size, B), F32)
        for k in range(size):
            pivot = jnp.broadcast_to(cols[k][k : k + 1, :], (size, B))
            rinv = 1.0 / pivot
            inv = jnp.where(row == k, rinv, inv)
            mult = jnp.where(row > k, cols[k] * rinv, 0.0)
            for j in range(k + 1, size):
                cols[j] = cols[j] - mult * cols[j][k : k + 1, :]
            left = left - mult * left[k : k + 1, :]
            right = right - mult * right[k : k + 1, :]
        w_ref[rows, 0:B] = left
        w_ref[rows, B : 2 * B] = right
        dv_ref[rows, :] = inv
        scaled = jnp.where(lane >= start + size, left * inv, 0.0)
        update = lax.dot_general(
            left6(scaled, 0),
            right6(jnp.concatenate([left, right], axis=1), 0),
            (((0,), (0,)), ((), ())),
            preferred_element_type=F32,
        )
        w_ref[...] = w_ref[...] - update
        return carry

    lax.fori_loop(first, last, block, 0)


def gather_kernel(
    step_ref,
    feat_ref,
    ls_hbm,
    noise_hbm,
    comp_ref,
    covar_ref,
    mrow_ref,
    colc_ref,
    pf_ref,
    ls_ref,
    noise_ref,
    comp_0,
    comp_1,
    comp_2,
    comp_3,
    feat_v,
    s_a,
    r_a,
    s_b,
    r_b,
    s_f,
    r_f,
    group,
    z_a,
    y_a,
    diag,
    ybuf,
    colcat,
    rowcat,
    rowc,
    w_v,
    dv_v,
    local_sem,
    send_sem,
    recv_sem,
):
    r = lax.axis_index("row")
    c = lax.axis_index("col")
    z = lax.rem(r, NZ)
    y = lax.div(r, NZ)
    axes = {
        "x": (c, NC, lambda i: (r, i)),
        "z": (z, NZ, lambda i: (y * NZ + i, c)),
        "y": (y, NY, lambda i: (i * NZ + z, c)),
    }
    partner = (y * NZ + c, z)
    sibling = c + 1 - 2 * lax.rem(c, 2)
    far = {8: (4, 3, 5, 2, 6, 1, 7), 4: (2, 1, 3)}
    near = {8: (1, 7, 2, 6, 3, 5, 4), 4: (1, 3, 2)}

    def other(me, d, n):
        return lax.rem(me + d, n)

    comp_v = (comp_0, comp_1, comp_2, comp_3)
    comp_copies = [
        pltpu.make_async_copy(comp_ref.at[pl.ds(k * B * KC, B * KC)], comp_v[k], local_sem.at[4 + k])
        for k in range(KR)
    ]
    feat_copy = pltpu.make_async_copy(feat_ref, feat_v, local_sem.at[0])
    ls_copy = pltpu.make_async_copy(ls_hbm, ls_ref, local_sem.at[1])
    noise_copy = pltpu.make_async_copy(noise_hbm, noise_ref, local_sem.at[2])
    for copy in comp_copies:
        copy.start()
    feat_copy.start()
    ls_copy.start()
    noise_copy.start()

    barrier = pltpu.get_barrier_semaphore()
    for me, n, dev in axes.values():
        for d in far[n]:
            pl.semaphore_signal(barrier, inc=1, device_id=dev(other(me, d, n)), device_id_type=MESH)

    @pl.when(z != c)
    def _():
        pl.semaphore_signal(barrier, inc=1, device_id=partner, device_id_type=MESH)

    def remote(src, dst, send, recv, dev):
        return pltpu.make_async_remote_copy(
            src_ref=src,
            dst_ref=dst,
            send_sem=send_sem.at[send],
            recv_sem=recv_sem.at[recv],
            device_id=dev,
            device_id_type=MESH,
        )

    waits = []

    def post(copy):
        copy.start()
        waits.append(copy)

    def spread(axis, src, dst, off, order=far):
        me, n, dev = axes[axis]
        for d in order[n]:
            peer = other(me, d, n)
            post(remote(src(peer), dst(me), off + d, off + me, dev(peer)))

    def arrived(axis, dst, off, steps=None):
        me, n, dev = axes[axis]
        for d in steps or near[n]:
            peer = other(me, d, n)
            remote(dst(peer), dst(peer), off + d, off + peer, dev(peer)).wait_recv()

    p = step_ref[0]
    panel_m = lax.div(p, NC)
    panel_c = lax.rem(p, NC)
    panel_k = lax.div(p, NR)
    panel_r = lax.rem(p, NR)
    panel_z = lax.rem(panel_r, NZ)
    panel_y = lax.div(panel_r, NZ)

    for k in range(KR):
        comp_copies[k].wait()
        block = comp_v[k][pl.ds(panel_m, B, stride=KC), :]
        s_b[:, k] = block.reshape(NC, PART, B)
    s_a[...] = s_b[:, panel_k]
    r_a[c] = s_a[c]
    r_b[c] = s_b[c]

    @pl.when(z != c)
    def _():
        pl.semaphore_wait(barrier, 2 * NC + NY - 2)

    @pl.when(z == c)
    def _():
        pl.semaphore_wait(barrier, 2 * NC + NY - 3)

    spread("x", lambda i: s_a.at[i], lambda i: r_a.at[i], 0)
    spread("x", lambda i: s_b.at[i], lambda i: r_b.at[i], 8)
    feat_copy.wait()
    ls_copy.wait()
    noise_copy.wait()

    part = pl.ds(pl.multiple_of(z * PART, PART), PART)
    feat_out = remote(feat_v.at[:, y, part, :], group.at[z, 6:10], 24, 24, partner)
    feat_in = remote(feat_v.at[:, y, part, :], group.at[c, 6:10], 24, 24, partner)

    @pl.when(z != c)
    def _():
        feat_out.start()

    @pl.when(z == c)
    def _():
        for k in range(KR):
            group[c, 6 + k] = feat_v[k, y, part, :]

    inv_ls = 1.0 / ls_ref[...]
    feat_p = feat_v[lax.div(panel_m, 4), lax.rem(panel_m, 4)] * inv_ls
    s_f[:, 0] = feat_p.reshape(NC, PART, B)
    noise_p = noise_ref[pl.ds(panel_m, 1), :]
    s_f[:, 1] = jnp.broadcast_to(noise_p.reshape(1, 1, B), (NC, PART, B))
    r_f[c] = s_f[c]
    spread("x", lambda i: s_f.at[i], lambda i: r_f.at[i], 16)

    def prepare(m, carry):
        pts = feat_v[lax.div(m, 4), lax.rem(m, 4)] * inv_ls
        colcat[pl.ds(pl.multiple_of(m * B, B), B), :] = operand(pts, False)
        return carry

    lax.fori_loop(0, KC // 2, prepare, 0, unroll=4)

    arrived("x", lambda i: r_a.at[i], 0)
    z_a[z] = r_a[panel_c]
    spread("z", lambda i: z_a.at[z], lambda i: z_a.at[i], 32)

    arrived("x", lambda i: r_b.at[i], 8)
    group[c, 0:4] = r_b[panel_c]
    move = remote(group.at[c, 0:4], ybuf.at[0, 0], 25, 25, partner)

    @pl.when(z != c)
    def _():
        move.start()

    @pl.when(z == c)
    def _():
        ybuf[0, 0] = group[c, 0:4]

    def over_y(rel):
        for d in near[NY]:
            peer = other(y, d, NY)
            slot = NY - d
            send = remote(
                ybuf.at[rel, 0], ybuf.at[rel, slot], 64 + rel * 4 + d, 64 + rel * 4 + slot, axes["y"][2](peer)
            )
            post(send)

    def from_y(rel):
        for d in near[NY]:
            peer = other(y, d, NY)
            here = ybuf.at[rel, d]
            remote(here, here, 64, 64 + rel * 4 + d, axes["y"][2](peer)).wait_recv()

    def over_z(d, quarter):
        peer = other(z, d, NZ)
        sem = 40 if quarter == 0 else 96 + 8 * (quarter - 1)
        post(
            remote(
                ybuf.at[0, quarter], ybuf.at[NZ - d, quarter], sem + d, sem + NZ - d, axes["z"][2](peer)
            )
        )

    def from_z(d, quarter):
        here = ybuf.at[d, quarter]
        sem = 40 if quarter == 0 else 96 + 8 * (quarter - 1)
        remote(here, here, sem, sem + d, axes["z"][2](other(z, d, NZ))).wait_recv()

    def relay(steps):
        for d in steps:
            from_z(d, 0)
            over_y(d)

    arrived("x", lambda i: r_f.at[i], 16)
    group[c, 4:6] = r_f[panel_c]

    @pl.when(z != c)
    def _():
        feat_in.wait_recv()

    mates = [(0, sibling)] + [(d, other(c, d, NC)) for d in (2, 6, 4)]
    for d, peer in mates[1:] + mates[:1]:
        post(remote(group.at[c], group.at[c], 120 + d, 120 + c, (r, peer)))
    lax.fori_loop(KC // 2, KC, prepare, 0, unroll=4)

    arrived("z", lambda i: z_a.at[i], 32)
    y_a[y] = z_a[panel_z]
    spread("y", lambda i: y_a.at[y], lambda i: y_a.at[i], 48)

    for d, peer in mates[1:]:
        slot = group.at[peer]
        remote(slot, slot, 120 + d, 120 + peer, (r, peer)).wait_recv()
        post(remote(slot, slot, 121 + d, 120 + peer, (r, sibling)))

    arrived("y", lambda i: y_a.at[i], 48)
    diag[c] = y_a[panel_y]
    spread("x", lambda i: diag.at[c], lambda i: diag.at[i], 56)

    @pl.when(z != c)
    def _():
        move.wait_recv()

    for d in near[NZ][:4]:
        over_z(d, 0)
    over_y(0)
    for d in near[NZ][4:]:
        over_z(d, 0)

    for d in (0, 2, 6, 4):
        slot = group.at[other(sibling, d, NC)]
        remote(slot, slot, 120, 120 + other(sibling, d, NC), (r, sibling)).wait_recv()

    for k in range(KR):
        rows = group[:, 6 + k].reshape(B, B)
        rowcat[k * B : (k + 1) * B, :] = operand(rows * inv_ls, True)
    eye = lax.broadcasted_iota(jnp.int32, (B, B), 0) == lax.broadcasted_iota(jnp.int32, (B, B), 1)

    def cover(quarter):
        for m2 in (2 * quarter, 2 * quarter + 1):
            expo = dot_nt(rowcat[...], colcat[m2 * 2 * B : (m2 + 1) * 2 * B, :])
            for j in range(2):
                m = m2 * 2 + j
                for k in range(KR):
                    value = jnp.exp(expo[k * B : (k + 1) * B, j * B : (j + 1) * B])
                    value = value + comp_v[k][pl.ds(m, B, stride=KC), :]
                    if m // 4 == k:
                        same = jnp.logical_and(z == c, y == m % 4)
                        value = value + jnp.where(jnp.logical_and(eye, same), noise_ref[m : m + 1, :], 0.0)
                    covar_ref[m, k * B : (k + 1) * B, :] = value

    cover(0)
    relay((1, 7))
    for d in near[NY]:
        here = ybuf.at[0, d]
        remote(here, here, 64, 64 + d, axes["y"][2](other(y, d, NY))).wait_recv()
        over_z(4, d)
    cover(1)
    relay((2, 6))

    pts_p = group[:, 4].reshape(B, B)
    left_p, right_p = operand(pts_p, True), operand(pts_p, False)
    noise_p = jnp.where(eye, group[0, 5, 0:1, :], 0.0)
    kernel_p = jnp.exp(dot_nt(left_p, right_p)) + noise_p
    kernel_row = jnp.exp(dot_nt(rowcat[...], right_p))
    for k in range(KR):
        here = k * NR + r == p
        raw = group[:, k].reshape(B, B)
        rowc[k * B : (k + 1) * B, :] = kernel_row[k * B : (k + 1) * B, :] + raw + jnp.where(here, noise_p, 0.0)

    arrived("x", lambda i: diag.at[i], 56)
    w_v[:, 0:B] = kernel_p + diag[...].reshape(B, B)
    w_v[:, B : 2 * B] = jnp.where(eye, 1.0, 0.0)
    eliminate(w_v, dv_v, 0, 4)
    relay((3, 5))
    eliminate(w_v, dv_v, 4, 8)
    linv = w_v[:, B : 2 * B] * jnp.sqrt(dv_v[...])
    dv_v[...] = linv
    solved = dot_nt(left6(rowc[...]), right6(linv))
    weights = jnp.dot(left6(solved), right6(linv, 0), preferred_element_type=F32)
    share = right6(dv_v[pl.ds(pl.multiple_of(c * PART, PART), PART), :])
    mine = dot_nt(share, left6(rowc[...]))
    row = lax.broadcasted_iota(jnp.int32, (PART, B), 1)
    col = lax.broadcasted_iota(jnp.int32, (PART, B), 0) + c * PART
    for k in range(KR):
        w = k * NR + r
        mrow_ref[k * B : (k + 1) * B, :] = jnp.where(w > p, weights[k * B : (k + 1) * B, :], 0.0)
        keep = jnp.logical_or(w > p, jnp.logical_and(w == p, col <= row))
        pf_ref[k] = jnp.where(keep, mine[:, k * B : (k + 1) * B], 0.0)

    def column(m, carry):
        rows = pl.ds(pl.multiple_of(m * B, B), B)
        colc_ref[rows, :] = jnp.exp(dot_nt(colcat[rows, :], left_p))
        return carry

    lax.fori_loop(0, KC, column, 0, unroll=8)
    cover(2)
    cover(3)

    for d in (1, 7, 2, 6, 3, 5):
        from_y(d)
    for quarter in range(NY):
        from_z(4, quarter)
    for rel in range(NY):
        for k in range(KR):
            m = k * 4 + other(y, rel, NY)
            raw = jnp.concatenate([ybuf[lax.rem(i + NZ - z, NZ), rel, k] for i in range(NZ)], axis=0)
            rows = pl.ds(pl.multiple_of(m * B, B), B)
            colc_ref[rows, :] = jnp.where(m * NC + c > p, colc_ref[rows, :] + raw, 0.0)

    for copy in waits:
        copy.wait_send()

    @pl.when(z != c)
    def _():
        feat_out.wait_send()
        move.wait_send()


def update_kernel(covar_ref, mrow_ref, colc_ref, pf_in, out_ref, pf_ref, out_v, sem):
    left = left4(mrow_ref[...])
    copies = []
    for half in range(2):
        for pair in range(2):
            rows = slice(pair * 2 * B, (pair + 1) * 2 * B)
            for m2 in range(half * 4, half * 4 + 4):
                update = dot_nt(left[rows, :], right4(colc_ref[m2 * 2 * B : (m2 + 1) * 2 * B, :]))
                for j in range(2):
                    m = m2 * 2 + j
                    value = covar_ref[m, rows, :] - update[:, j * B : (j + 1) * B]
                    out_v[pl.ds(pair * 2 * B * KC + m, 2 * B, stride=KC), :] = value
            view = out_v.reshape(KR * B, KC, B)
            part = (pl.ds(pair * 2 * B, 2 * B), pl.ds(half * 8, 8))
            copy = pltpu.make_async_copy(view.at[part], out_ref.at[part], sem.at[half * 2 + pair])
            copy.start()
            copies.append(copy)
    pf_ref[...] = pf_in[...]
    for copy in copies:
        copy.wait()


def in_hbm(x):
    return pltpu.with_memory_space_constraint(x, pltpu.HBM)


def body(features, lengthscales, noise_var, component, step_index):
    hbm = pl.BlockSpec(memory_space=pltpu.HBM)
    vmem = pl.BlockSpec(memory_space=pltpu.VMEM)
    smem = pl.BlockSpec(memory_space=pltpu.SMEM)
    covar, mrow, colc, pf = pl.pallas_call(
        gather_kernel,
        out_shape=(
            jax.ShapeDtypeStruct((KC, KR * B, B), F32),
            jax.ShapeDtypeStruct((KR * B, B), F32),
            jax.ShapeDtypeStruct((KC * B, B), F32),
            jax.ShapeDtypeStruct((KR, PART, B), F32),
        ),
        in_specs=[smem, hbm, hbm, hbm, hbm],
        out_specs=(vmem, vmem, vmem, vmem),
        scratch_shapes=[
            pltpu.VMEM((1, B), F32),
            pltpu.VMEM((KC, B), F32),
            pltpu.VMEM((B * KC, B), F32),
            pltpu.VMEM((B * KC, B), F32),
            pltpu.VMEM((B * KC, B), F32),
            pltpu.VMEM((B * KC, B), F32),
            pltpu.VMEM((4, 4, B, B), F32),
            pltpu.VMEM((NC, PART, B), F32),
            pltpu.VMEM((NC, PART, B), F32),
            pltpu.VMEM((NC, KR, PART, B), F32),
            pltpu.VMEM((NC, KR, PART, B), F32),
            pltpu.VMEM((NC, 2, PART, B), F32),
            pltpu.VMEM((NC, 2, PART, B), F32),
            pltpu.VMEM((NC, GROUP, PART, B), F32),
            pltpu.VMEM((NZ, PART, B), F32),
            pltpu.VMEM((NY, PART, B), F32),
            pltpu.VMEM((NC, PART, B), F32),
            pltpu.VMEM((NZ, NY, KR, PART, B), F32),
            pltpu.VMEM((KC * B, DEPTH), BF16),
            pltpu.VMEM((KR * B, DEPTH), BF16),
            pltpu.VMEM((KR * B, B), F32),
            pltpu.VMEM((B, 2 * B), F32),
            pltpu.VMEM((B, B), F32),
            pltpu.SemaphoreType.DMA((8,)),
            pltpu.SemaphoreType.DMA((136,)),
            pltpu.SemaphoreType.DMA((136,)),
        ],
        compiler_params=pltpu.CompilerParams(
            collective_id=0, has_side_effects=True, vmem_limit_bytes=GATHER_VMEM
        ),
        name="gather_panel",
    )(
        step_index,
        in_hbm(features.reshape(4, 4, B, B)),
        in_hbm(lengthscales.reshape(1, B)),
        in_hbm(noise_var),
        in_hbm(component.reshape(KR * B * KC, B)),
    )
    trailing, pf = pl.pallas_call(
        update_kernel,
        out_shape=(
            jax.ShapeDtypeStruct((KR * B, KC, B), F32),
            jax.ShapeDtypeStruct((KR, PART, B), F32),
        ),
        in_specs=[vmem, vmem, vmem, vmem],
        out_specs=(hbm, vmem),
        scratch_shapes=[
            pltpu.VMEM((KR * B * KC, B), F32),
            pltpu.SemaphoreType.DMA((4,)),
        ],
        compiler_params=pltpu.CompilerParams(vmem_limit_bytes=UPDATE_VMEM),
        name="update_blocks",
    )(covar, mrow, colc, pf)
    return jnp.swapaxes(pf, 1, 2), trailing.reshape(KR, B, KC, B)


def solution(mesh):
    in_specs = (P(None, "col", None), P(), P(None, "col"), P(None, "row", None, "col"), P())
    out_specs = (P(None, "row", "col"), P(None, "row", None, "col"))
    return jax.shard_map(body, mesh=mesh, in_specs=in_specs, out_specs=out_specs, check_vma=False)
```

```python
import functools

import jax
import jax.numpy as jnp
from jax import lax
from jax.experimental import pallas as pl
from jax.experimental.pallas import tpu as pltpu
from jax.sharding import PartitionSpec as P

MESH = pl.DeviceIdType.MESH
F32 = jnp.float32
BF16 = jnp.bfloat16
B = 128
KR, KC, NR, NC = 4, 16, 32, 8
NY, NZ = 4, 8
PART = B // NC
GROUP = 2 * KR + 2
DEPTH = 5 * B
GATHER_VMEM = 40 * 1024 * 1024
UPDATE_VMEM = 16 * 1024 * 1024


def split2(x):
    high = x.astype(BF16)
    return high, (x - high.astype(F32)).astype(BF16)


def split3(x):
    high = x.astype(BF16)
    rest = x - high.astype(F32)
    mid = rest.astype(BF16)
    low = (rest - mid.astype(F32)).astype(BF16)
    return high, mid, low


def left4(x):
    h, m = split2(x)
    return jnp.concatenate([h, h, m, m], axis=1)


def right4(x):
    h, m = split2(x)
    return jnp.concatenate([h, m, h, m], axis=1)


def left6(x, axis=1):
    h, m, l = split3(x)
    return jnp.concatenate([h, h, m, h, m, l], axis=axis)


def right6(x, axis=1):
    h, m, l = split3(x)
    return jnp.concatenate([h, m, h, l, m, h], axis=axis)


def dot_nt(a, b):
    return lax.dot_general(a, b, (((1,), (1,)), ((), ())), preferred_element_type=F32)


def operand(points, is_left):
    h, m = split2(points)
    rounded = h.astype(F32) + m.astype(F32)
    half = -0.5 * jnp.sum(rounded * rounded, axis=1, keepdims=True)
    pieces = [jnp.broadcast_to(v.astype(F32), points.shape) for v in split3(half)]
    lane = lax.broadcasted_iota(jnp.int32, points.shape, 1)
    first = 3 if is_left else 0
    extra = jnp.where(lane < 6, 1.0, 0.0)
    for i, piece in enumerate(pieces):
        extra = jnp.where(lane == first + i, piece, extra)
    extra = extra.astype(BF16)
    if is_left:
        return jnp.concatenate([h, h, m, m, extra], axis=1)
    return jnp.concatenate([h, m, h, m, extra], axis=1)


def eliminate(w_ref, dv_ref):
    size = 16
    lane = lax.broadcasted_iota(jnp.int32, (size, B), 1)
    row = lax.broadcasted_iota(jnp.int32, (size, B), 0)

    def block(b, carry):
        start = pl.multiple_of(b * size, size)
        rows = pl.ds(start, size)
        left = w_ref[rows, 0:B]
        right = w_ref[rows, B : 2 * B]
        rolled = pltpu.roll(left, lax.rem(B - start, B), axis=1)
        cols = [jnp.broadcast_to(rolled[:, k : k + 1], (size, B)) for k in range(size)]
        inv = jnp.zeros((size, B), F32)
        for k in range(size):
            pivot = jnp.broadcast_to(cols[k][k : k + 1, :], (size, B))
            rinv = 1.0 / pivot
            inv = jnp.where(row == k, rinv, inv)
            mult = jnp.where(row > k, cols[k] * rinv, 0.0)
            for j in range(k + 1, size):
                cols[j] = cols[j] - mult * cols[j][k : k + 1, :]
            left = left - mult * left[k : k + 1, :]
            right = right - mult * right[k : k + 1, :]
        w_ref[rows, 0:B] = left
        w_ref[rows, B : 2 * B] = right
        dv_ref[rows, :] = inv
        scaled = jnp.where(lane >= start + size, left * inv, 0.0)
        update = lax.dot_general(
            left6(scaled, 0),
            right6(jnp.concatenate([left, right], axis=1), 0),
            (((0,), (0,)), ((), ())),
            preferred_element_type=F32,
        )
        w_ref[...] = w_ref[...] - update
        return carry

    lax.fori_loop(0, B // size, block, 0)


def gather_kernel(
    step_ref,
    feat_ref,
    ls_hbm,
    noise_hbm,
    comp_ref,
    covar_ref,
    mrow_ref,
    colc_ref,
    pf_ref,
    ls_ref,
    noise_ref,
    comp_0,
    comp_1,
    comp_2,
    comp_3,
    feat_v,
    s_a,
    r_a,
    s_b,
    r_b,
    s_f,
    r_f,
    group,
    z_a,
    y_a,
    diag,
    ybuf,
    colcat,
    rowcat,
    rowc,
    w_v,
    dv_v,
    local_sem,
    send_sem,
    recv_sem,
):
    r = lax.axis_index("row")
    c = lax.axis_index("col")
    z = lax.rem(r, NZ)
    y = lax.div(r, NZ)
    axes = {
        "x": (c, NC, lambda i: (r, i)),
        "z": (z, NZ, lambda i: (y * NZ + i, c)),
        "y": (y, NY, lambda i: (i * NZ + z, c)),
    }
    sibling = c + 1 - 2 * lax.rem(c, 2)
    shifts = ((4, 3), (1, 2), (0, 7), (6, 5))

    def shift_of(chips, core):
        total = 0
        for e in range(4):
            for h in range(2):
                total = total + jnp.where(jnp.logical_and(chips == e, core == h), shifts[e][h], 0)
        return total

    def part_at(shift, plane):
        total = 0
        for e in range(4):
            for h in range(2):
                part = lax.rem(lax.div(plane, 2) + e, 4) * 2 + h
                total = total + jnp.where(shift == shifts[e][h], part, 0)
        return total

    chips = lax.rem(lax.div(c, 2) + 4 - lax.div(z, 2), 4)
    to_row = lax.rem(z + shift_of(chips, lax.rem(c, 2)), NZ)
    target = (y * NZ + to_row, z)
    source_part = part_at(lax.rem(z + NZ - c, NZ), c)
    source = (y * NZ + c, source_part)
    far = {8: (4, 3, 5, 2, 6, 1, 7), 4: (2, 1, 3)}
    near = {8: (1, 7, 2, 6, 3, 5, 4), 4: (1, 3, 2)}

    def other(me, d, n):
        return lax.rem(me + d, n)

    comp_v = (comp_0, comp_1, comp_2, comp_3)
    comp_copies = [
        pltpu.make_async_copy(comp_ref.at[pl.ds(k * B * KC, B * KC)], comp_v[k], local_sem.at[4 + k])
        for k in range(KR)
    ]
    feat_copy = pltpu.make_async_copy(feat_ref, feat_v, local_sem.at[0])
    ls_copy = pltpu.make_async_copy(ls_hbm, ls_ref, local_sem.at[1])
    noise_copy = pltpu.make_async_copy(noise_hbm, noise_ref, local_sem.at[2])
    for copy in comp_copies:
        copy.start()
    feat_copy.start()
    ls_copy.start()
    noise_copy.start()

    barrier = pltpu.get_barrier_semaphore()
    for me, n, dev in axes.values():
        for d in far[n]:
            pl.semaphore_signal(barrier, inc=1, device_id=dev(other(me, d, n)), device_id_type=MESH)

    pl.semaphore_signal(barrier, inc=1, device_id=source, device_id_type=MESH)
    pl.semaphore_signal(barrier, inc=1, device_id=target, device_id_type=MESH)

    def remote(src, dst, send, recv, dev):
        return pltpu.make_async_remote_copy(
            src_ref=src,
            dst_ref=dst,
            send_sem=send_sem.at[send],
            recv_sem=recv_sem.at[recv],
            device_id=dev,
            device_id_type=MESH,
        )

    waits = []

    def post(copy):
        copy.start()
        waits.append(copy)

    def spread(axis, src, dst, off, order=far):
        me, n, dev = axes[axis]
        for d in order[n]:
            peer = other(me, d, n)
            post(remote(src(peer), dst(me), off + d, off + me, dev(peer)))

    def arrived(axis, dst, off, steps=None):
        me, n, dev = axes[axis]
        for d in steps or near[n]:
            peer = other(me, d, n)
            remote(dst(peer), dst(peer), off + d, off + peer, dev(peer)).wait_recv()

    p = step_ref[0]
    panel_m = lax.div(p, NC)
    panel_c = lax.rem(p, NC)
    panel_k = lax.div(p, NR)
    panel_r = lax.rem(p, NR)
    panel_z = lax.rem(panel_r, NZ)
    panel_y = lax.div(panel_r, NZ)

    for k in range(KR):
        comp_copies[k].wait()
        block = comp_v[k][pl.ds(panel_m, B, stride=KC), :]
        s_b[:, k] = block.reshape(NC, PART, B)
    s_a[...] = s_b[:, panel_k]
    r_a[c] = s_a[c]
    r_b[c] = s_b[c]

    pl.semaphore_wait(barrier, 2 * NC + NY - 1)

    spread("x", lambda i: s_a.at[i], lambda i: r_a.at[i], 0)
    spread("x", lambda i: s_b.at[i], lambda i: r_b.at[i], 8)
    feat_copy.wait()
    ls_copy.wait()
    noise_copy.wait()

    part = pl.ds(pl.multiple_of(source_part * PART, PART), PART)
    feat_out = remote(feat_v.at[:, y, part, :], group.at[source_part, 6:10], 24, 24, source)
    feat_in = remote(feat_v.at[:, y, part, :], group.at[c, 6:10], 24, 24, source)
    post(feat_out)

    inv_ls = 1.0 / ls_ref[...]
    feat_p = feat_v[lax.div(panel_m, 4), lax.rem(panel_m, 4)] * inv_ls
    s_f[:, 0] = feat_p.reshape(NC, PART, B)
    noise_p = noise_ref[pl.ds(panel_m, 1), :]
    s_f[:, 1] = jnp.broadcast_to(noise_p.reshape(1, 1, B), (NC, PART, B))
    r_f[c] = s_f[c]
    spread("x", lambda i: s_f.at[i], lambda i: r_f.at[i], 16)

    def prepare(m, carry):
        pts = feat_v[lax.div(m, 4), lax.rem(m, 4)] * inv_ls
        colcat[pl.ds(pl.multiple_of(m * B, B), B), :] = operand(pts, False)
        return carry

    lax.fori_loop(0, KC // 2, prepare, 0, unroll=4)

    arrived("x", lambda i: r_a.at[i], 0)
    z_a[z] = r_a[panel_c]
    spread("z", lambda i: z_a.at[z], lambda i: z_a.at[i], 32)

    arrived("x", lambda i: r_b.at[i], 8)
    group[c, 0:4] = r_b[panel_c]
    move = remote(group.at[c, 0:4], ybuf.at[0, 0], 25, 25, target)
    post(move)

    late = (3, 4, 5)

    def over_y(rel):
        for d in near[NY]:
            if d == 2 and rel not in late:
                continue
            peer = other(y, d, NY)
            slot = NY - d
            post(
                remote(
                    ybuf.at[rel, 0], ybuf.at[rel, slot], 64 + rel * 4 + d, 64 + rel * 4 + slot, axes["y"][2](peer)
                )
            )

    def over_y2(rel):
        side = 3 if rel % 2 == 0 else 1
        from_y(rel, (side,))
        post(
            remote(
                ybuf.at[rel, side],
                ybuf.at[rel, 2],
                64 + rel * 4 + 2,
                64 + rel * 4 + 2,
                axes["y"][2](other(y, NY - side, NY)),
            )
        )

    def from_y(rel, sides):
        for d in sides:
            here = ybuf.at[rel, d]
            remote(here, here, 64, 64 + rel * 4 + d, axes["y"][2](other(y, d, NY))).wait_recv()

    def over_z(rel, d, send):
        slot = (rel - d) % NZ
        post(remote(ybuf.at[rel, 0], ybuf.at[slot, 0], 40 + send, 40 + slot, axes["z"][2](other(z, d, NZ))))

    def from_z(d):
        here = ybuf.at[d, 0]
        remote(here, here, 40, 40 + d, axes["z"][2](other(z, d, NZ))).wait_recv()

    arrived("x", lambda i: r_f.at[i], 16)
    group[c, 4:6] = r_f[panel_c]
    feat_in.wait_recv()

    mates = [(0, sibling)] + [(d, other(c, d, NC)) for d in (2, 6, 4)]
    for d, peer in mates[1:] + mates[:1]:
        post(remote(group.at[c], group.at[c], 120 + d, 120 + c, (r, peer)))
    lax.fori_loop(KC // 2, KC, prepare, 0, unroll=4)

    arrived("z", lambda i: z_a.at[i], 32)
    y_a[y] = z_a[panel_z]
    spread("y", lambda i: y_a.at[y], lambda i: y_a.at[i], 48)

    move.wait_recv()
    for send, d in enumerate((1, 7, 2, 6)):
        over_z(0, d, 1 + send)
    over_y(0)

    for d, peer in mates[1:]:
        slot = group.at[peer]
        remote(slot, slot, 120 + d, 120 + peer, (r, peer)).wait_recv()
        post(remote(slot, slot, 121 + d, 120 + peer, (r, sibling)))

    arrived("y", lambda i: y_a.at[i], 48)
    diag[c] = y_a[panel_y]
    spread("x", lambda i: diag.at[c], lambda i: diag.at[i], 56)

    for d in (1, 7):
        from_z(d)
    from_z(6)
    over_z(6, 1, 5)
    over_z(6, 2, 6)
    from_z(2)
    over_z(2, 7, 7)
    for rel in (1, 7, 6, 2):
        over_y(rel)
    over_y2(0)

    for d in (0, 2, 6, 4):
        slot = group.at[other(sibling, d, NC)]
        remote(slot, slot, 120, 120 + other(sibling, d, NC), (r, sibling)).wait_recv()

    for k in range(KR):
        rows = group[:, 6 + k].reshape(B, B)
        rowcat[k * B : (k + 1) * B, :] = operand(rows * inv_ls, True)
    eye = lax.broadcasted_iota(jnp.int32, (B, B), 0) == lax.broadcasted_iota(jnp.int32, (B, B), 1)

    def cover(quarter):
        for m2 in (2 * quarter, 2 * quarter + 1):
            expo = dot_nt(rowcat[...], colcat[m2 * 2 * B : (m2 + 1) * 2 * B, :])
            for j in range(2):
                m = m2 * 2 + j
                for k in range(KR):
                    value = jnp.exp(expo[k * B : (k + 1) * B, j * B : (j + 1) * B])
                    value = value + comp_v[k][pl.ds(m, B, stride=KC), :]
                    if m // 4 == k:
                        same = jnp.logical_and(z == c, y == m % 4)
                        value = value + jnp.where(jnp.logical_and(eye, same), noise_ref[m : m + 1, :], 0.0)
                    covar_ref[m, k * B : (k + 1) * B, :] = value

    cover(0)
    for rel in (1, 7):
        over_y2(rel)
    for rel in (5, 3, 4):
        from_z(rel)
        over_y(rel)
    cover(1)
    for rel in (6, 2):
        over_y2(rel)
    cover(2)

    pts_p = group[:, 4].reshape(B, B)
    left_p, right_p = operand(pts_p, True), operand(pts_p, False)
    noise_p = jnp.where(eye, group[0, 5, 0:1, :], 0.0)
    kernel_p = jnp.exp(dot_nt(left_p, right_p)) + noise_p
    kernel_row = jnp.exp(dot_nt(rowcat[...], right_p))
    for k in range(KR):
        here = k * NR + r == p
        raw = group[:, k].reshape(B, B)
        value = kernel_row[k * B : (k + 1) * B, :] + raw + jnp.where(here, noise_p, 0.0)
        rowc[k * B : (k + 1) * B, :] = left6(value)

    arrived("x", lambda i: diag.at[i], 56)
    w_v[:, 0:B] = kernel_p + diag[...].reshape(B, B)
    w_v[:, B : 2 * B] = jnp.where(eye, 1.0, 0.0)
    eliminate(w_v, dv_v)
    linv = w_v[:, B : 2 * B] * jnp.sqrt(dv_v[...])
    dv_v[...] = linv
    inverse = lax.dot_general(
        left6(linv, 0), right6(linv, 0), (((0,), (0,)), ((), ())), preferred_element_type=F32
    )
    weights = dot_nt(rowc[...], right6(inverse))
    share = right6(dv_v[pl.ds(pl.multiple_of(c * PART, PART), PART), :])
    mine = dot_nt(share, rowc[...])
    row = lax.broadcasted_iota(jnp.int32, (PART, B), 1)
    col = lax.broadcasted_iota(jnp.int32, (PART, B), 0) + c * PART
    for k in range(KR):
        w = k * NR + r
        mrow_ref[k * B : (k + 1) * B, :] = jnp.where(w > p, weights[k * B : (k + 1) * B, :], 0.0)
        keep = jnp.logical_or(w > p, jnp.logical_and(w == p, col <= row))
        pf_ref[k] = jnp.where(keep, mine[:, k * B : (k + 1) * B], 0.0)

    def column(m, carry):
        rows = pl.ds(pl.multiple_of(m * B, B), B)
        colc_ref[rows, :] = jnp.exp(dot_nt(colcat[rows, :], left_p))
        return carry

    lax.fori_loop(0, KC, column, 0, unroll=8)
    cover(3)

    for rel in (0, 1, 7, 6, 2):
        from_y(rel, (2, 1) if rel % 2 == 0 else (2, 3))
    for rel in late:
        from_y(rel, near[NY])
    places = [
        lax.rem(c + shift_of(lax.rem(i // 2 + 4 - lax.div(c, 2), 4), i % 2) + NZ - z, NZ) for i in range(NC)
    ]
    for rel in range(NY):
        for k in range(KR):
            m = k * 4 + other(y, rel, NY)
            raw = jnp.concatenate([ybuf[place, rel, k] for place in places], axis=0)
            rows = pl.ds(pl.multiple_of(m * B, B), B)
            colc_ref[rows, :] = jnp.where(m * NC + c > p, colc_ref[rows, :] + raw, 0.0)

    for copy in waits:
        copy.wait_send()


def update_kernel(covar_ref, mrow_ref, colc_ref, pf_in, out_ref, pf_ref, out_v, sem):
    left = left4(mrow_ref[...])
    copies = []
    for half in range(2):
        for pair in range(2):
            rows = slice(pair * 2 * B, (pair + 1) * 2 * B)
            for m2 in range(half * 4, half * 4 + 4):
                update = dot_nt(left[rows, :], right4(colc_ref[m2 * 2 * B : (m2 + 1) * 2 * B, :]))
                for j in range(2):
                    m = m2 * 2 + j
                    value = covar_ref[m, rows, :] - update[:, j * B : (j + 1) * B]
                    out_v[pl.ds(pair * 2 * B * KC + m, 2 * B, stride=KC), :] = value
            view = out_v.reshape(KR * B, KC, B)
            part = (pl.ds(pair * 2 * B, 2 * B), pl.ds(half * 8, 8))
            copy = pltpu.make_async_copy(view.at[part], out_ref.at[part], sem.at[half * 2 + pair])
            copy.start()
            copies.append(copy)
    pf_ref[...] = pf_in[...]
    for copy in copies:
        copy.wait()


def in_hbm(x):
    return pltpu.with_memory_space_constraint(x, pltpu.HBM)


def body(features, lengthscales, noise_var, component, step_index):
    hbm = pl.BlockSpec(memory_space=pltpu.HBM)
    vmem = pl.BlockSpec(memory_space=pltpu.VMEM)
    smem = pl.BlockSpec(memory_space=pltpu.SMEM)
    covar, mrow, colc, pf = pl.pallas_call(
        gather_kernel,
        out_shape=(
            jax.ShapeDtypeStruct((KC, KR * B, B), F32),
            jax.ShapeDtypeStruct((KR * B, B), F32),
            jax.ShapeDtypeStruct((KC * B, B), F32),
            jax.ShapeDtypeStruct((KR, PART, B), F32),
        ),
        in_specs=[smem, hbm, hbm, hbm, hbm],
        out_specs=(vmem, vmem, vmem, vmem),
        scratch_shapes=[
            pltpu.VMEM((1, B), F32),
            pltpu.VMEM((KC, B), F32),
            pltpu.VMEM((B * KC, B), F32),
            pltpu.VMEM((B * KC, B), F32),
            pltpu.VMEM((B * KC, B), F32),
            pltpu.VMEM((B * KC, B), F32),
            pltpu.VMEM((4, 4, B, B), F32),
            pltpu.VMEM((NC, PART, B), F32),
            pltpu.VMEM((NC, PART, B), F32),
            pltpu.VMEM((NC, KR, PART, B), F32),
            pltpu.VMEM((NC, KR, PART, B), F32),
            pltpu.VMEM((NC, 2, PART, B), F32),
            pltpu.VMEM((NC, 2, PART, B), F32),
            pltpu.VMEM((NC, GROUP, PART, B), F32),
            pltpu.VMEM((NZ, PART, B), F32),
            pltpu.VMEM((NY, PART, B), F32),
            pltpu.VMEM((NC, PART, B), F32),
            pltpu.VMEM((NZ, NY, KR, PART, B), F32),
            pltpu.VMEM((KC * B, DEPTH), BF16),
            pltpu.VMEM((KR * B, DEPTH), BF16),
            pltpu.VMEM((KR * B, 6 * B), BF16),
            pltpu.VMEM((B, 2 * B), F32),
            pltpu.VMEM((B, B), F32),
            pltpu.SemaphoreType.DMA((8,)),
            pltpu.SemaphoreType.DMA((136,)),
            pltpu.SemaphoreType.DMA((136,)),
        ],
        compiler_params=pltpu.CompilerParams(
            collective_id=0, has_side_effects=True, vmem_limit_bytes=GATHER_VMEM
        ),
        name="gather_panel",
    )(
        step_index,
        in_hbm(features.reshape(4, 4, B, B)),
        in_hbm(lengthscales.reshape(1, B)),
        in_hbm(noise_var),
        in_hbm(component.reshape(KR * B * KC, B)),
    )
    trailing, pf = pl.pallas_call(
        update_kernel,
        out_shape=(
            jax.ShapeDtypeStruct((KR * B, KC, B), F32),
            jax.ShapeDtypeStruct((KR, PART, B), F32),
        ),
        in_specs=[vmem, vmem, vmem, vmem],
        out_specs=(hbm, vmem),
        scratch_shapes=[
            pltpu.VMEM((KR * B * KC, B), F32),
            pltpu.SemaphoreType.DMA((4,)),
        ],
        compiler_params=pltpu.CompilerParams(vmem_limit_bytes=UPDATE_VMEM),
        name="update_blocks",
    )(covar, mrow, colc, pf)
    return jnp.swapaxes(pf, 1, 2), trailing.reshape(KR, B, KC, B)


def solution(mesh):
    in_specs = (P(None, "col", None), P(), P(None, "col"), P(None, "row", None, "col"), P())
    out_specs = (P(None, "row", "col"), P(None, "row", None, "col"))
    return jax.shard_map(body, mesh=mesh, in_specs=in_specs, out_specs=out_specs, check_vma=False)
```

```python
import functools

import jax
import jax.numpy as jnp
from jax import lax
from jax.experimental import pallas as pl
from jax.experimental.pallas import tpu as pltpu
from jax.sharding import PartitionSpec as P

MESH = pl.DeviceIdType.MESH
F32 = jnp.float32
BF16 = jnp.bfloat16
B = 128
KR, KC, NR, NC = 4, 16, 32, 8
NY, NZ = 4, 8
PART = B // NC
GROUP = 2 * KR + 2
DEPTH = 5 * B
GATHER_VMEM = 40 * 1024 * 1024
UPDATE_VMEM = 16 * 1024 * 1024


def split2(x):
    high = x.astype(BF16)
    return high, (x - high.astype(F32)).astype(BF16)


def split3(x):
    high = x.astype(BF16)
    rest = x - high.astype(F32)
    mid = rest.astype(BF16)
    low = (rest - mid.astype(F32)).astype(BF16)
    return high, mid, low


def left4(x):
    h, m = split2(x)
    return jnp.concatenate([h, h, m, m], axis=1)


def right4(x):
    h, m = split2(x)
    return jnp.concatenate([h, m, h, m], axis=1)


def left6(x, axis=1):
    h, m, l = split3(x)
    return jnp.concatenate([h, h, m, h, m, l], axis=axis)


def right6(x, axis=1):
    h, m, l = split3(x)
    return jnp.concatenate([h, m, h, l, m, h], axis=axis)


def dot_nt(a, b):
    return lax.dot_general(a, b, (((1,), (1,)), ((), ())), preferred_element_type=F32)


def operand(points, is_left):
    h, m = split2(points)
    rounded = h.astype(F32) + m.astype(F32)
    half = -0.5 * jnp.sum(rounded * rounded, axis=1, keepdims=True)
    pieces = [jnp.broadcast_to(v.astype(F32), points.shape) for v in split3(half)]
    lane = lax.broadcasted_iota(jnp.int32, points.shape, 1)
    first = 3 if is_left else 0
    extra = jnp.where(lane < 6, 1.0, 0.0)
    for i, piece in enumerate(pieces):
        extra = jnp.where(lane == first + i, piece, extra)
    extra = extra.astype(BF16)
    if is_left:
        return jnp.concatenate([h, h, m, m, extra], axis=1)
    return jnp.concatenate([h, m, h, m, extra], axis=1)


def eliminate(w_ref, dv_ref, between):
    size = 16
    lane = lax.broadcasted_iota(jnp.int32, (size, B), 1)
    row = lax.broadcasted_iota(jnp.int32, (size, B), 0)
    for start in range(0, B, size):
        rows = slice(start, start + size)
        left = w_ref[rows, 0:B]
        right = w_ref[rows, B : 2 * B]
        cols = [jnp.broadcast_to(left[:, start + k : start + k + 1], (size, B)) for k in range(size)]
        inv = jnp.zeros((size, B), F32)
        for k in range(size):
            rinv = 1.0 / jnp.broadcast_to(cols[k][k : k + 1, :], (size, B))
            inv = jnp.where(row == k, rinv, inv)
            mult = jnp.where(row > k, cols[k] * rinv, 0.0)
            for j in range(k + 1, size):
                cols[j] = cols[j] - mult * cols[j][k : k + 1, :]
            left = left - mult * left[k : k + 1, :]
            right = right - mult * right[k : k + 1, :]
        w_ref[rows, 0:B] = left
        w_ref[rows, B : 2 * B] = right
        dv_ref[rows, :] = inv
        end = start + size
        if end < B:
            scaled = jnp.where(lane >= end, left * inv, 0.0)
            update = lax.dot_general(
                left6(scaled, 0),
                right6(jnp.concatenate([left, right], axis=1), 0),
                (((0,), (0,)), ((), ())),
                preferred_element_type=F32,
            )
            w_ref[end:, :] = w_ref[end:, :] - update[end:, :]
        between(end // size)


def gather_kernel(
    step_ref,
    feat_ref,
    ls_hbm,
    noise_hbm,
    comp_ref,
    covar_ref,
    mrow_ref,
    colc_ref,
    pf_ref,
    ls_ref,
    noise_ref,
    comp_0,
    comp_1,
    comp_2,
    comp_3,
    feat_v,
    s_a,
    r_a,
    s_b,
    r_b,
    s_f,
    r_f,
    group,
    z_a,
    y_a,
    diag,
    ybuf,
    colcat,
    rowcat,
    rowc,
    w_v,
    dv_v,
    local_sem,
    send_sem,
    recv_sem,
):
    r = lax.axis_index("row")
    c = lax.axis_index("col")
    z = lax.rem(r, NZ)
    y = lax.div(r, NZ)
    axes = {
        "x": (c, NC, lambda i: (r, i)),
        "z": (z, NZ, lambda i: (y * NZ + i, c)),
        "y": (y, NY, lambda i: (i * NZ + z, c)),
    }
    sibling = c + 1 - 2 * lax.rem(c, 2)
    shifts = ((4, 3), (1, 2), (0, 7), (6, 5))

    def shift_of(chips, core):
        total = 0
        for e in range(4):
            for h in range(2):
                total = total + jnp.where(jnp.logical_and(chips == e, core == h), shifts[e][h], 0)
        return total

    def part_at(shift, plane):
        total = 0
        for e in range(4):
            for h in range(2):
                part = lax.rem(lax.div(plane, 2) + e, 4) * 2 + h
                total = total + jnp.where(shift == shifts[e][h], part, 0)
        return total

    chips = lax.rem(lax.div(c, 2) + 4 - lax.div(z, 2), 4)
    to_row = lax.rem(z + shift_of(chips, lax.rem(c, 2)), NZ)
    target = (y * NZ + to_row, z)
    source_part = part_at(lax.rem(z + NZ - c, NZ), c)
    source = (y * NZ + c, source_part)
    far = {8: (4, 3, 5, 2, 6, 1, 7), 4: (2, 1, 3)}
    near = {8: (1, 7, 2, 6, 3, 5, 4), 4: (1, 3, 2)}

    def other(me, d, n):
        return lax.rem(me + d, n)

    comp_v = (comp_0, comp_1, comp_2, comp_3)
    comp_copies = [
        pltpu.make_async_copy(comp_ref.at[pl.ds(k * B * KC, B * KC)], comp_v[k], local_sem.at[4 + k])
        for k in range(KR)
    ]
    feat_copy = pltpu.make_async_copy(feat_ref, feat_v, local_sem.at[0])
    ls_copy = pltpu.make_async_copy(ls_hbm, ls_ref, local_sem.at[1])
    noise_copy = pltpu.make_async_copy(noise_hbm, noise_ref, local_sem.at[2])
    for copy in comp_copies:
        copy.start()
    feat_copy.start()
    ls_copy.start()
    noise_copy.start()

    barrier = pltpu.get_barrier_semaphore()
    for me, n, dev in axes.values():
        for d in far[n]:
            pl.semaphore_signal(barrier, inc=1, device_id=dev(other(me, d, n)), device_id_type=MESH)

    pl.semaphore_signal(barrier, inc=1, device_id=source, device_id_type=MESH)
    pl.semaphore_signal(barrier, inc=1, device_id=target, device_id_type=MESH)

    def remote(src, dst, send, recv, dev):
        return pltpu.make_async_remote_copy(
            src_ref=src,
            dst_ref=dst,
            send_sem=send_sem.at[send],
            recv_sem=recv_sem.at[recv],
            device_id=dev,
            device_id_type=MESH,
        )

    waits = []

    def post(copy):
        copy.start()
        waits.append(copy)

    def spread(axis, src, dst, off, order=far):
        me, n, dev = axes[axis]
        for d in order[n]:
            peer = other(me, d, n)
            post(remote(src(peer), dst(me), off + d, off + me, dev(peer)))

    def arrived(axis, dst, off, steps=None):
        me, n, dev = axes[axis]
        for d in steps or near[n]:
            peer = other(me, d, n)
            remote(dst(peer), dst(peer), off + d, off + peer, dev(peer)).wait_recv()

    p = step_ref[0]
    panel_m = lax.div(p, NC)
    panel_c = lax.rem(p, NC)
    panel_k = lax.div(p, NR)
    panel_r = lax.rem(p, NR)
    panel_z = lax.rem(panel_r, NZ)
    panel_y = lax.div(panel_r, NZ)

    for k in range(KR):
        comp_copies[k].wait()
        block = comp_v[k][pl.ds(panel_m, B, stride=KC), :]
        s_b[:, k] = block.reshape(NC, PART, B)
    s_a[...] = s_b[:, panel_k]
    r_a[c] = s_a[c]
    r_b[c] = s_b[c]

    pl.semaphore_wait(barrier, 2 * NC + NY - 1)

    spread("x", lambda i: s_a.at[i], lambda i: r_a.at[i], 0)
    spread("x", lambda i: s_b.at[i], lambda i: r_b.at[i], 8)
    feat_copy.wait()
    ls_copy.wait()
    noise_copy.wait()

    part = pl.ds(pl.multiple_of(source_part * PART, PART), PART)
    feat_out = remote(feat_v.at[:, y, part, :], group.at[source_part, 6:10], 24, 24, source)
    feat_in = remote(feat_v.at[:, y, part, :], group.at[c, 6:10], 24, 24, source)
    post(feat_out)

    inv_ls = 1.0 / ls_ref[...]
    feat_p = feat_v[lax.div(panel_m, 4), lax.rem(panel_m, 4)] * inv_ls
    s_f[:, 0] = feat_p.reshape(NC, PART, B)
    noise_p = noise_ref[pl.ds(panel_m, 1), :]
    s_f[:, 1] = jnp.broadcast_to(noise_p.reshape(1, 1, B), (NC, PART, B))
    r_f[c] = s_f[c]
    spread("x", lambda i: s_f.at[i], lambda i: r_f.at[i], 16)

    def prepare(m, carry):
        pts = feat_v[lax.div(m, 4), lax.rem(m, 4)] * inv_ls
        colcat[pl.ds(pl.multiple_of(m * B, B), B), :] = operand(pts, False)
        return carry

    lax.fori_loop(0, KC // 2, prepare, 0, unroll=4)

    arrived("x", lambda i: r_a.at[i], 0)
    z_a[z] = r_a[panel_c]
    spread("z", lambda i: z_a.at[z], lambda i: z_a.at[i], 32)

    arrived("x", lambda i: r_b.at[i], 8)
    group[c, 0:4] = r_b[panel_c]
    move = remote(group.at[c, 0:4], ybuf.at[0, 0], 25, 25, target)
    post(move)

    def over_y(rel):
        for d in near[NY]:
            peer = other(y, d, NY)
            slot = NY - d
            post(
                remote(
                    ybuf.at[rel, 0], ybuf.at[rel, slot], 64 + rel * 4 + d, 64 + rel * 4 + slot, axes["y"][2](peer)
                )
            )

    def from_y(rel):
        for d in near[NY]:
            here = ybuf.at[rel, d]
            remote(here, here, 64, 64 + rel * 4 + d, axes["y"][2](other(y, d, NY))).wait_recv()

    def over_z(d):
        post(remote(ybuf.at[0, 0], ybuf.at[NZ - d, 0], 40 + d, 40 + NZ - d, axes["z"][2](other(z, d, NZ))))

    def from_z(d):
        here = ybuf.at[d, 0]
        remote(here, here, 40, 40 + d, axes["z"][2](other(z, d, NZ))).wait_recv()

    arrived("x", lambda i: r_f.at[i], 16)
    group[c, 4:6] = r_f[panel_c]
    feat_in.wait_recv()

    mates = [(0, sibling)] + [(d, other(c, d, NC)) for d in (2, 6, 4)]
    for d, peer in mates[1:] + mates[:1]:
        post(remote(group.at[c], group.at[c], 120 + d, 120 + c, (r, peer)))
    lax.fori_loop(KC // 2, KC, prepare, 0, unroll=4)

    arrived("z", lambda i: z_a.at[i], 32)
    y_a[y] = z_a[panel_z]
    spread("y", lambda i: y_a.at[y], lambda i: y_a.at[i], 48)

    move.wait_recv()
    for d in near[NZ][:4]:
        over_z(d)
    over_y(0)
    for d in near[NZ][4:]:
        over_z(d)

    for d, peer in mates[1:]:
        slot = group.at[peer]
        remote(slot, slot, 120 + d, 120 + peer, (r, peer)).wait_recv()
        post(remote(slot, slot, 121 + d, 120 + peer, (r, sibling)))

    arrived("y", lambda i: y_a.at[i], 48)
    diag[c] = y_a[panel_y]
    spread("x", lambda i: diag.at[c], lambda i: diag.at[i], 56)

    def relay(*rels):
        for rel in rels:
            from_z(rel)
            over_y(rel)

    relay(1, 7)
    for d in (0, 2, 6, 4):
        slot = group.at[other(sibling, d, NC)]
        remote(slot, slot, 120, 120 + other(sibling, d, NC), (r, sibling)).wait_recv()

    for k in range(KR):
        rows = group[:, 6 + k].reshape(B, B)
        rowcat[k * B : (k + 1) * B, :] = operand(rows * inv_ls, True)
    eye = lax.broadcasted_iota(jnp.int32, (B, B), 0) == lax.broadcasted_iota(jnp.int32, (B, B), 1)

    def cover(quarter):
        for m2 in (2 * quarter, 2 * quarter + 1):
            expo = dot_nt(rowcat[...], colcat[m2 * 2 * B : (m2 + 1) * 2 * B, :])
            for j in range(2):
                m = m2 * 2 + j
                for k in range(KR):
                    value = jnp.exp(expo[k * B : (k + 1) * B, j * B : (j + 1) * B])
                    value = value + comp_v[k][pl.ds(m, B, stride=KC), :]
                    if m // 4 == k:
                        same = jnp.logical_and(z == c, y == m % 4)
                        value = value + jnp.where(jnp.logical_and(eye, same), noise_ref[m : m + 1, :], 0.0)
                    covar_ref[m, k * B : (k + 1) * B, :] = value

    cover(0)
    relay(2, 6)
    cover(1)

    pts_p = group[:, 4].reshape(B, B)
    left_p, right_p = operand(pts_p, True), operand(pts_p, False)
    noise_p = jnp.where(eye, group[0, 5, 0:1, :], 0.0)
    kernel_p = jnp.exp(dot_nt(left_p, right_p)) + noise_p
    kernel_row = jnp.exp(dot_nt(rowcat[...], right_p))
    for k in range(KR):
        here = k * NR + r == p
        raw = group[:, k].reshape(B, B)
        value = kernel_row[k * B : (k + 1) * B, :] + raw + jnp.where(here, noise_p, 0.0)
        rowc[k * B : (k + 1) * B, :] = left6(value)

    arrived("x", lambda i: diag.at[i], 56)
    w_v[:, 0:B] = kernel_p + diag[...].reshape(B, B)
    w_v[:, B : 2 * B] = jnp.where(eye, 1.0, 0.0)

    def between(done):
        if done == 2:
            relay(3, 5)
        if done == 4:
            relay(4)

    eliminate(w_v, dv_v, between)
    linv = w_v[:, B : 2 * B] * jnp.sqrt(dv_v[...])
    dv_v[...] = linv
    inverse = lax.dot_general(
        left6(linv, 0), right6(linv, 0), (((0,), (0,)), ((), ())), preferred_element_type=F32
    )
    weights = dot_nt(rowc[...], right6(inverse))
    share = right6(dv_v[pl.ds(pl.multiple_of(c * PART, PART), PART), :])
    mine = dot_nt(share, rowc[...])
    row = lax.broadcasted_iota(jnp.int32, (PART, B), 1)
    col = lax.broadcasted_iota(jnp.int32, (PART, B), 0) + c * PART
    for k in range(KR):
        w = k * NR + r
        mrow_ref[k * B : (k + 1) * B, :] = jnp.where(w > p, weights[k * B : (k + 1) * B, :], 0.0)
        keep = jnp.logical_or(w > p, jnp.logical_and(w == p, col <= row))
        pf_ref[k] = jnp.where(keep, mine[:, k * B : (k + 1) * B], 0.0)

    def column(m, carry):
        rows = pl.ds(pl.multiple_of(m * B, B), B)
        colc_ref[rows, :] = jnp.exp(dot_nt(colcat[rows, :], left_p))
        return carry

    lax.fori_loop(0, KC, column, 0, unroll=8)
    cover(2)
    cover(3)

    for rel in range(NZ):
        from_y(rel)
    places = [
        lax.rem(c + shift_of(lax.rem(i // 2 + 4 - lax.div(c, 2), 4), i % 2) + NZ - z, NZ) for i in range(NC)
    ]
    for rel in range(NY):
        for k in range(KR):
            m = k * 4 + other(y, rel, NY)
            raw = jnp.concatenate([ybuf[place, rel, k] for place in places], axis=0)
            rows = pl.ds(pl.multiple_of(m * B, B), B)
            colc_ref[rows, :] = jnp.where(m * NC + c > p, colc_ref[rows, :] + raw, 0.0)

    for copy in waits:
        copy.wait_send()


def update_kernel(covar_ref, mrow_ref, colc_ref, pf_in, out_ref, pf_ref, out_v, sem):
    left = left4(mrow_ref[...])
    copies = []
    for half in range(2):
        for pair in range(2):
            rows = slice(pair * 2 * B, (pair + 1) * 2 * B)
            for m2 in range(half * 4, half * 4 + 4):
                update = dot_nt(left[rows, :], right4(colc_ref[m2 * 2 * B : (m2 + 1) * 2 * B, :]))
                for j in range(2):
                    m = m2 * 2 + j
                    value = covar_ref[m, rows, :] - update[:, j * B : (j + 1) * B]
                    out_v[pl.ds(pair * 2 * B * KC + m, 2 * B, stride=KC), :] = value
            view = out_v.reshape(KR * B, KC, B)
            part = (pl.ds(pair * 2 * B, 2 * B), pl.ds(half * 8, 8))
            copy = pltpu.make_async_copy(view.at[part], out_ref.at[part], sem.at[half * 2 + pair])
            copy.start()
            copies.append(copy)
    pf_ref[...] = pf_in[...]
    for copy in copies:
        copy.wait()


def in_hbm(x):
    return pltpu.with_memory_space_constraint(x, pltpu.HBM)


def body(features, lengthscales, noise_var, component, step_index):
    hbm = pl.BlockSpec(memory_space=pltpu.HBM)
    vmem = pl.BlockSpec(memory_space=pltpu.VMEM)
    smem = pl.BlockSpec(memory_space=pltpu.SMEM)
    covar, mrow, colc, pf = pl.pallas_call(
        gather_kernel,
        out_shape=(
            jax.ShapeDtypeStruct((KC, KR * B, B), F32),
            jax.ShapeDtypeStruct((KR * B, B), F32),
            jax.ShapeDtypeStruct((KC * B, B), F32),
            jax.ShapeDtypeStruct((KR, PART, B), F32),
        ),
        in_specs=[smem, hbm, hbm, hbm, hbm],
        out_specs=(vmem, vmem, vmem, vmem),
        scratch_shapes=[
            pltpu.VMEM((1, B), F32),
            pltpu.VMEM((KC, B), F32),
            pltpu.VMEM((B * KC, B), F32),
            pltpu.VMEM((B * KC, B), F32),
            pltpu.VMEM((B * KC, B), F32),
            pltpu.VMEM((B * KC, B), F32),
            pltpu.VMEM((4, 4, B, B), F32),
            pltpu.VMEM((NC, PART, B), F32),
            pltpu.VMEM((NC, PART, B), F32),
            pltpu.VMEM((NC, KR, PART, B), F32),
            pltpu.VMEM((NC, KR, PART, B), F32),
            pltpu.VMEM((NC, 2, PART, B), F32),
            pltpu.VMEM((NC, 2, PART, B), F32),
            pltpu.VMEM((NC, GROUP, PART, B), F32),
            pltpu.VMEM((NZ, PART, B), F32),
            pltpu.VMEM((NY, PART, B), F32),
            pltpu.VMEM((NC, PART, B), F32),
            pltpu.VMEM((NZ, NY, KR, PART, B), F32),
            pltpu.VMEM((KC * B, DEPTH), BF16),
            pltpu.VMEM((KR * B, DEPTH), BF16),
            pltpu.VMEM((KR * B, 6 * B), BF16),
            pltpu.VMEM((B, 2 * B), F32),
            pltpu.VMEM((B, B), F32),
            pltpu.SemaphoreType.DMA((8,)),
            pltpu.SemaphoreType.DMA((136,)),
            pltpu.SemaphoreType.DMA((136,)),
        ],
        compiler_params=pltpu.CompilerParams(
            collective_id=0, has_side_effects=True, vmem_limit_bytes=GATHER_VMEM
        ),
        name="gather_panel",
    )(
        step_index,
        in_hbm(features.reshape(4, 4, B, B)),
        in_hbm(lengthscales.reshape(1, B)),
        in_hbm(noise_var),
        in_hbm(component.reshape(KR * B * KC, B)),
    )
    trailing, pf = pl.pallas_call(
        update_kernel,
        out_shape=(
            jax.ShapeDtypeStruct((KR * B, KC, B), F32),
            jax.ShapeDtypeStruct((KR, PART, B), F32),
        ),
        in_specs=[vmem, vmem, vmem, vmem],
        out_specs=(hbm, vmem),
        scratch_shapes=[
            pltpu.VMEM((KR * B * KC, B), F32),
            pltpu.SemaphoreType.DMA((4,)),
        ],
        compiler_params=pltpu.CompilerParams(vmem_limit_bytes=UPDATE_VMEM),
        name="update_blocks",
    )(covar, mrow, colc, pf)
    return jnp.swapaxes(pf, 1, 2), trailing.reshape(KR, B, KC, B)


def solution(mesh):
    in_specs = (P(None, "col", None), P(), P(None, "col"), P(None, "row", None, "col"), P())
    out_specs = (P(None, "row", "col"), P(None, "row", None, "col"))
    return jax.shard_map(body, mesh=mesh, in_specs=in_specs, out_specs=out_specs, check_vma=False)
```

```python
import functools

import jax
import jax.numpy as jnp
from jax import lax
from jax.experimental import pallas as pl
from jax.experimental.pallas import tpu as pltpu
from jax.sharding import PartitionSpec as P

MESH = pl.DeviceIdType.MESH
F32 = jnp.float32
BF16 = jnp.bfloat16
B = 128
KR, KC, NR, NC = 4, 16, 32, 8
NY, NZ = 4, 8
PART = B // NC
GROUP = 2 * KR + 2
DEPTH = 5 * B
GATHER_VMEM = 40 * 1024 * 1024
UPDATE_VMEM = 16 * 1024 * 1024


def split2(x):
    high = x.astype(BF16)
    return high, (x - high.astype(F32)).astype(BF16)


def split3(x):
    high = x.astype(BF16)
    rest = x - high.astype(F32)
    mid = rest.astype(BF16)
    low = (rest - mid.astype(F32)).astype(BF16)
    return high, mid, low


def left4(x):
    h, m = split2(x)
    return jnp.concatenate([h, h, m, m], axis=1)


def right4(x):
    h, m = split2(x)
    return jnp.concatenate([h, m, h, m], axis=1)


def left6(x, axis=1):
    h, m, l = split3(x)
    return jnp.concatenate([h, h, m, h, m, l], axis=axis)


def right6(x, axis=1):
    h, m, l = split3(x)
    return jnp.concatenate([h, m, h, l, m, h], axis=axis)


def dot_nt(a, b):
    return lax.dot_general(a, b, (((1,), (1,)), ((), ())), preferred_element_type=F32)


def operand(points, is_left):
    h, m = split2(points)
    rounded = h.astype(F32) + m.astype(F32)
    half = -0.5 * jnp.sum(rounded * rounded, axis=1, keepdims=True)
    pieces = [jnp.broadcast_to(v.astype(F32), points.shape) for v in split3(half)]
    lane = lax.broadcasted_iota(jnp.int32, points.shape, 1)
    first = 3 if is_left else 0
    extra = jnp.where(lane < 6, 1.0, 0.0)
    for i, piece in enumerate(pieces):
        extra = jnp.where(lane == first + i, piece, extra)
    extra = extra.astype(BF16)
    if is_left:
        return jnp.concatenate([h, h, m, m, extra], axis=1)
    return jnp.concatenate([h, m, h, m, extra], axis=1)


def eliminate(w_ref, dv_ref, between):
    size = 16
    lane = lax.broadcasted_iota(jnp.int32, (size, B), 1)
    row = lax.broadcasted_iota(jnp.int32, (size, B), 0)
    for start in range(0, B, size):
        rows = slice(start, start + size)
        left = w_ref[rows, 0:B]
        right = w_ref[rows, B : 2 * B]
        cols = [jnp.broadcast_to(left[:, start + k : start + k + 1], (size, B)) for k in range(size)]
        inv = jnp.zeros((size, B), F32)
        for k in range(size):
            rinv = 1.0 / jnp.broadcast_to(cols[k][k : k + 1, :], (size, B))
            inv = jnp.where(row == k, rinv, inv)
            mult = jnp.where(row > k, cols[k] * rinv, 0.0)
            for j in range(k + 1, size):
                cols[j] = cols[j] - mult * cols[j][k : k + 1, :]
            left = left - mult * left[k : k + 1, :]
            right = right - mult * right[k : k + 1, :]
        w_ref[rows, 0:B] = left
        w_ref[rows, B : 2 * B] = right
        dv_ref[rows, :] = inv
        end = start + size
        if end < B:
            scaled = jnp.where(lane >= end, left * inv, 0.0)
            update = lax.dot_general(
                left6(scaled, 0),
                right6(jnp.concatenate([left, right], axis=1), 0),
                (((0,), (0,)), ((), ())),
                preferred_element_type=F32,
            )
            w_ref[end:, :] = w_ref[end:, :] - update[end:, :]
        between(end // size)


def gather_kernel(
    step_ref,
    feat_ref,
    ls_hbm,
    noise_hbm,
    comp_ref,
    covar_ref,
    mrow_ref,
    colc_ref,
    pf_ref,
    ls_ref,
    noise_ref,
    comp_0,
    comp_1,
    comp_2,
    comp_3,
    feat_v,
    s_a,
    r_a,
    s_b,
    r_b,
    s_f,
    r_f,
    group,
    z_a,
    y_a,
    diag,
    ybuf,
    colcat,
    rowcat,
    rowc,
    w_v,
    dv_v,
    local_sem,
    send_sem,
    recv_sem,
):
    r = lax.axis_index("row")
    c = lax.axis_index("col")
    z = lax.rem(r, NZ)
    y = lax.div(r, NZ)
    axes = {
        "x": (c, NC, lambda i: (r, i)),
        "z": (z, NZ, lambda i: (y * NZ + i, c)),
        "y": (y, NY, lambda i: (i * NZ + z, c)),
    }
    sibling = c + 1 - 2 * lax.rem(c, 2)
    shifts = ((4, 3), (1, 2), (0, 7), (6, 5))

    def shift_of(chips, core):
        total = 0
        for e in range(4):
            for h in range(2):
                total = total + jnp.where(jnp.logical_and(chips == e, core == h), shifts[e][h], 0)
        return total

    def part_at(shift, plane):
        total = 0
        for e in range(4):
            for h in range(2):
                part = lax.rem(lax.div(plane, 2) + e, 4) * 2 + h
                total = total + jnp.where(shift == shifts[e][h], part, 0)
        return total

    chips = lax.rem(lax.div(c, 2) + 4 - lax.div(z, 2), 4)
    to_row = lax.rem(z + shift_of(chips, lax.rem(c, 2)), NZ)
    target = (y * NZ + to_row, z)
    source_part = part_at(lax.rem(z + NZ - c, NZ), c)
    source = (y * NZ + c, source_part)
    far = {8: (4, 3, 5, 2, 6, 1, 7), 4: (2, 1, 3)}
    near = {8: (1, 7, 2, 6, 3, 5, 4), 4: (1, 3, 2)}

    def other(me, d, n):
        return lax.rem(me + d, n)

    comp_v = (comp_0, comp_1, comp_2, comp_3)
    comp_copies = [
        pltpu.make_async_copy(comp_ref.at[pl.ds(k * B * KC, B * KC)], comp_v[k], local_sem.at[4 + k])
        for k in range(KR)
    ]
    feat_copy = pltpu.make_async_copy(feat_ref, feat_v, local_sem.at[0])
    ls_copy = pltpu.make_async_copy(ls_hbm, ls_ref, local_sem.at[1])
    noise_copy = pltpu.make_async_copy(noise_hbm, noise_ref, local_sem.at[2])
    for copy in comp_copies:
        copy.start()
    feat_copy.start()
    ls_copy.start()
    noise_copy.start()

    barrier = pltpu.get_barrier_semaphore()
    for me, n, dev in axes.values():
        for d in far[n]:
            pl.semaphore_signal(barrier, inc=1, device_id=dev(other(me, d, n)), device_id_type=MESH)

    pl.semaphore_signal(barrier, inc=1, device_id=source, device_id_type=MESH)
    pl.semaphore_signal(barrier, inc=1, device_id=target, device_id_type=MESH)

    def remote(src, dst, send, recv, dev):
        return pltpu.make_async_remote_copy(
            src_ref=src,
            dst_ref=dst,
            send_sem=send_sem.at[send],
            recv_sem=recv_sem.at[recv],
            device_id=dev,
            device_id_type=MESH,
        )

    waits = []

    def post(copy):
        copy.start()
        waits.append(copy)

    def spread(axis, src, dst, off, order=far):
        me, n, dev = axes[axis]
        for d in order[n]:
            peer = other(me, d, n)
            post(remote(src(peer), dst(me), off + d, off + me, dev(peer)))

    def arrived(axis, dst, off, steps=None):
        me, n, dev = axes[axis]
        for d in steps or near[n]:
            peer = other(me, d, n)
            remote(dst(peer), dst(peer), off + d, off + peer, dev(peer)).wait_recv()

    p = step_ref[0]
    panel_m = lax.div(p, NC)
    panel_c = lax.rem(p, NC)
    panel_k = lax.div(p, NR)
    panel_r = lax.rem(p, NR)
    panel_z = lax.rem(panel_r, NZ)
    panel_y = lax.div(panel_r, NZ)

    for k in range(KR):
        comp_copies[k].wait()
        block = comp_v[k][pl.ds(panel_m, B, stride=KC), :]
        s_b[:, k] = block.reshape(NC, PART, B)
    s_a[...] = s_b[:, panel_k]
    r_a[c] = s_a[c]
    r_b[c] = s_b[c]

    pl.semaphore_wait(barrier, 2 * NC + NY - 1)

    spread("x", lambda i: s_a.at[i], lambda i: r_a.at[i], 0)
    spread("x", lambda i: s_b.at[i], lambda i: r_b.at[i], 8)
    feat_copy.wait()
    ls_copy.wait()
    noise_copy.wait()

    part = pl.ds(pl.multiple_of(source_part * PART, PART), PART)
    feat_out = remote(feat_v.at[:, y, part, :], group.at[source_part, 6:10], 24, 24, source)
    feat_in = remote(feat_v.at[:, y, part, :], group.at[c, 6:10], 24, 24, source)
    post(feat_out)

    inv_ls = 1.0 / ls_ref[...]
    feat_p = feat_v[lax.div(panel_m, 4), lax.rem(panel_m, 4)] * inv_ls
    s_f[:, 0] = feat_p.reshape(NC, PART, B)
    noise_p = noise_ref[pl.ds(panel_m, 1), :]
    s_f[:, 1] = jnp.broadcast_to(noise_p.reshape(1, 1, B), (NC, PART, B))
    r_f[c] = s_f[c]
    spread("x", lambda i: s_f.at[i], lambda i: r_f.at[i], 16)

    def prepare(m, carry):
        pts = feat_v[lax.div(m, 4), lax.rem(m, 4)] * inv_ls
        colcat[pl.ds(pl.multiple_of(m * B, B), B), :] = operand(pts, False)
        return carry

    lax.fori_loop(0, KC // 2, prepare, 0, unroll=4)

    arrived("x", lambda i: r_a.at[i], 0)
    z_a[z] = r_a[panel_c]
    spread("z", lambda i: z_a.at[z], lambda i: z_a.at[i], 32)

    arrived("x", lambda i: r_b.at[i], 8)
    group[c, 0:4] = r_b[panel_c]
    move = remote(group.at[c, 0:4], ybuf.at[0, 0], 25, 25, target)
    post(move)

    def over_y(rel):
        for d in near[NY]:
            peer = other(y, d, NY)
            slot = NY - d
            post(
                remote(
                    ybuf.at[rel, 0], ybuf.at[rel, slot], 64 + rel * 4 + d, 64 + rel * 4 + slot, axes["y"][2](peer)
                )
            )

    def from_y(rel):
        for d in near[NY]:
            here = ybuf.at[rel, d]
            remote(here, here, 64, 64 + rel * 4 + d, axes["y"][2](other(y, d, NY))).wait_recv()

    def over_z(d):
        post(remote(ybuf.at[0, 0], ybuf.at[NZ - d, 0], 40 + d, 40 + NZ - d, axes["z"][2](other(z, d, NZ))))

    def over_z4(slot):
        post(remote(ybuf.at[0, slot], ybuf.at[4, slot], 96 + slot, 96 + slot, axes["z"][2](other(z, 4, NZ))))

    def from_z(d):
        here = ybuf.at[d, 0]
        remote(here, here, 40, 40 + d, axes["z"][2](other(z, d, NZ))).wait_recv()

    arrived("x", lambda i: r_f.at[i], 16)
    group[c, 4:6] = r_f[panel_c]
    feat_in.wait_recv()

    mates = [(0, sibling)] + [(d, other(c, d, NC)) for d in (2, 6, 4)]
    for d, peer in mates[1:] + mates[:1]:
        post(remote(group.at[c], group.at[c], 120 + d, 120 + c, (r, peer)))
    lax.fori_loop(KC // 2, KC, prepare, 0, unroll=4)

    arrived("z", lambda i: z_a.at[i], 32)
    y_a[y] = z_a[panel_z]
    spread("y", lambda i: y_a.at[y], lambda i: y_a.at[i], 48)

    move.wait_recv()
    for d in near[NZ][:4]:
        over_z(d)
    over_y(0)
    for d in near[NZ][4:]:
        over_z(d)

    for d, peer in mates[1:]:
        slot = group.at[peer]
        remote(slot, slot, 120 + d, 120 + peer, (r, peer)).wait_recv()
        post(remote(slot, slot, 121 + d, 120 + peer, (r, sibling)))

    arrived("y", lambda i: y_a.at[i], 48)
    diag[c] = y_a[panel_y]
    spread("x", lambda i: diag.at[c], lambda i: diag.at[i], 56)

    def relay(*rels):
        for rel in rels:
            from_z(rel)
            over_y(rel)

    relay(1, 7)
    for d in (0, 2, 6, 4):
        slot = group.at[other(sibling, d, NC)]
        remote(slot, slot, 120, 120 + other(sibling, d, NC), (r, sibling)).wait_recv()

    for k in range(KR):
        rows = group[:, 6 + k].reshape(B, B)
        rowcat[k * B : (k + 1) * B, :] = operand(rows * inv_ls, True)
    eye = lax.broadcasted_iota(jnp.int32, (B, B), 0) == lax.broadcasted_iota(jnp.int32, (B, B), 1)

    def cover(quarter):
        for m2 in (2 * quarter, 2 * quarter + 1):
            expo = dot_nt(rowcat[...], colcat[m2 * 2 * B : (m2 + 1) * 2 * B, :])
            for j in range(2):
                m = m2 * 2 + j
                for k in range(KR):
                    value = jnp.exp(expo[k * B : (k + 1) * B, j * B : (j + 1) * B])
                    value = value + comp_v[k][pl.ds(m, B, stride=KC), :]
                    if m // 4 == k:
                        same = jnp.logical_and(z == c, y == m % 4)
                        value = value + jnp.where(jnp.logical_and(eye, same), noise_ref[m : m + 1, :], 0.0)
                    covar_ref[m, k * B : (k + 1) * B, :] = value

    cover(0)
    from_y(0)
    for slot in range(1, NY):
        over_z4(slot)
    relay(2, 6)
    cover(1)
    cover(2)

    pts_p = group[:, 4].reshape(B, B)
    left_p, right_p = operand(pts_p, True), operand(pts_p, False)
    noise_p = jnp.where(eye, group[0, 5, 0:1, :], 0.0)
    kernel_p = jnp.exp(dot_nt(left_p, right_p)) + noise_p
    kernel_row = jnp.exp(dot_nt(rowcat[...], right_p))
    for k in range(KR):
        here = k * NR + r == p
        raw = group[:, k].reshape(B, B)
        value = kernel_row[k * B : (k + 1) * B, :] + raw + jnp.where(here, noise_p, 0.0)
        rowc[k * B : (k + 1) * B, :] = left6(value)

    arrived("x", lambda i: diag.at[i], 56)
    w_v[:, 0:B] = kernel_p + diag[...].reshape(B, B)
    w_v[:, B : 2 * B] = jnp.where(eye, 1.0, 0.0)

    def between(done):
        if done == 2:
            relay(3, 5)

    eliminate(w_v, dv_v, between)
    linv = w_v[:, B : 2 * B] * jnp.sqrt(dv_v[...])
    dv_v[...] = linv
    inverse = lax.dot_general(
        left6(linv, 0), right6(linv, 0), (((0,), (0,)), ((), ())), preferred_element_type=F32
    )
    weights = dot_nt(rowc[...], right6(inverse))
    share = right6(dv_v[pl.ds(pl.multiple_of(c * PART, PART), PART), :])
    mine = dot_nt(share, rowc[...])
    row = lax.broadcasted_iota(jnp.int32, (PART, B), 1)
    col = lax.broadcasted_iota(jnp.int32, (PART, B), 0) + c * PART
    for k in range(KR):
        w = k * NR + r
        mrow_ref[k * B : (k + 1) * B, :] = jnp.where(w > p, weights[k * B : (k + 1) * B, :], 0.0)
        keep = jnp.logical_or(w > p, jnp.logical_and(w == p, col <= row))
        pf_ref[k] = jnp.where(keep, mine[:, k * B : (k + 1) * B], 0.0)

    def column(m, carry):
        rows = pl.ds(pl.multiple_of(m * B, B), B)
        colc_ref[rows, :] = jnp.exp(dot_nt(colcat[rows, :], left_p))
        return carry

    lax.fori_loop(0, KC, column, 0, unroll=8)
    cover(3)

    for rel in (1, 7, 2, 6, 3, 5):
        from_y(rel)
    from_z(4)
    for slot in range(1, NY):
        far_z = ybuf.at[4, slot]
        remote(far_z, far_z, 96, 96 + slot, axes["z"][2](other(z, 4, NZ))).wait_recv()
    places = [
        lax.rem(c + shift_of(lax.rem(i // 2 + 4 - lax.div(c, 2), 4), i % 2) + NZ - z, NZ) for i in range(NC)
    ]
    for rel in range(NY):
        for k in range(KR):
            m = k * 4 + other(y, rel, NY)
            raw = jnp.concatenate([ybuf[place, rel, k] for place in places], axis=0)
            rows = pl.ds(pl.multiple_of(m * B, B), B)
            colc_ref[rows, :] = jnp.where(m * NC + c > p, colc_ref[rows, :] + raw, 0.0)

    for copy in waits:
        copy.wait_send()


def update_kernel(covar_ref, mrow_ref, colc_ref, pf_in, out_ref, pf_ref, out_v, sem):
    left = left4(mrow_ref[...])
    copies = []
    for half in range(2):
        for pair in range(2):
            rows = slice(pair * 2 * B, (pair + 1) * 2 * B)
            for m2 in range(half * 4, half * 4 + 4):
                update = dot_nt(left[rows, :], right4(colc_ref[m2 * 2 * B : (m2 + 1) * 2 * B, :]))
                for j in range(2):
                    m = m2 * 2 + j
                    value = covar_ref[m, rows, :] - update[:, j * B : (j + 1) * B]
                    out_v[pl.ds(pair * 2 * B * KC + m, 2 * B, stride=KC), :] = value
            view = out_v.reshape(KR * B, KC, B)
            part = (pl.ds(pair * 2 * B, 2 * B), pl.ds(half * 8, 8))
            copy = pltpu.make_async_copy(view.at[part], out_ref.at[part], sem.at[half * 2 + pair])
            copy.start()
            copies.append(copy)
    pf_ref[...] = pf_in[...]
    for copy in copies:
        copy.wait()


def in_hbm(x):
    return pltpu.with_memory_space_constraint(x, pltpu.HBM)


def body(features, lengthscales, noise_var, component, step_index):
    hbm = pl.BlockSpec(memory_space=pltpu.HBM)
    vmem = pl.BlockSpec(memory_space=pltpu.VMEM)
    smem = pl.BlockSpec(memory_space=pltpu.SMEM)
    covar, mrow, colc, pf = pl.pallas_call(
        gather_kernel,
        out_shape=(
            jax.ShapeDtypeStruct((KC, KR * B, B), F32),
            jax.ShapeDtypeStruct((KR * B, B), F32),
            jax.ShapeDtypeStruct((KC * B, B), F32),
            jax.ShapeDtypeStruct((KR, PART, B), F32),
        ),
        in_specs=[smem, hbm, hbm, hbm, hbm],
        out_specs=(vmem, vmem, vmem, vmem),
        scratch_shapes=[
            pltpu.VMEM((1, B), F32),
            pltpu.VMEM((KC, B), F32),
            pltpu.VMEM((B * KC, B), F32),
            pltpu.VMEM((B * KC, B), F32),
            pltpu.VMEM((B * KC, B), F32),
            pltpu.VMEM((B * KC, B), F32),
            pltpu.VMEM((4, 4, B, B), F32),
            pltpu.VMEM((NC, PART, B), F32),
            pltpu.VMEM((NC, PART, B), F32),
            pltpu.VMEM((NC, KR, PART, B), F32),
            pltpu.VMEM((NC, KR, PART, B), F32),
            pltpu.VMEM((NC, 2, PART, B), F32),
            pltpu.VMEM((NC, 2, PART, B), F32),
            pltpu.VMEM((NC, GROUP, PART, B), F32),
            pltpu.VMEM((NZ, PART, B), F32),
            pltpu.VMEM((NY, PART, B), F32),
            pltpu.VMEM((NC, PART, B), F32),
            pltpu.VMEM((NZ, NY, KR, PART, B), F32),
            pltpu.VMEM((KC * B, DEPTH), BF16),
            pltpu.VMEM((KR * B, DEPTH), BF16),
            pltpu.VMEM((KR * B, 6 * B), BF16),
            pltpu.VMEM((B, 2 * B), F32),
            pltpu.VMEM((B, B), F32),
            pltpu.SemaphoreType.DMA((8,)),
            pltpu.SemaphoreType.DMA((136,)),
            pltpu.SemaphoreType.DMA((136,)),
        ],
        compiler_params=pltpu.CompilerParams(
            collective_id=0, has_side_effects=True, vmem_limit_bytes=GATHER_VMEM
        ),
        name="gather_panel",
    )(
        step_index,
        in_hbm(features.reshape(4, 4, B, B)),
        in_hbm(lengthscales.reshape(1, B)),
        in_hbm(noise_var),
        in_hbm(component.reshape(KR * B * KC, B)),
    )
    trailing, pf = pl.pallas_call(
        update_kernel,
        out_shape=(
            jax.ShapeDtypeStruct((KR * B, KC, B), F32),
            jax.ShapeDtypeStruct((KR, PART, B), F32),
        ),
        in_specs=[vmem, vmem, vmem, vmem],
        out_specs=(hbm, vmem),
        scratch_shapes=[
            pltpu.VMEM((KR * B * KC, B), F32),
            pltpu.SemaphoreType.DMA((4,)),
        ],
        compiler_params=pltpu.CompilerParams(vmem_limit_bytes=UPDATE_VMEM),
        name="update_blocks",
    )(covar, mrow, colc, pf)
    return jnp.swapaxes(pf, 1, 2), trailing.reshape(KR, B, KC, B)


def solution(mesh):
    in_specs = (P(None, "col", None), P(), P(None, "col"), P(None, "row", None, "col"), P())
    out_specs = (P(None, "row", "col"), P(None, "row", None, "col"))
    return jax.shard_map(body, mesh=mesh, in_specs=in_specs, out_specs=out_specs, check_vma=False)
```

```python
import functools

import jax
import jax.numpy as jnp
from jax import lax
from jax.experimental import pallas as pl
from jax.experimental.pallas import tpu as pltpu
from jax.sharding import PartitionSpec as P

MESH = pl.DeviceIdType.MESH
F32 = jnp.float32
BF16 = jnp.bfloat16
B = 128
KR, KC, NR, NC = 4, 16, 32, 8
NY, NZ = 4, 8
PART = B // NC
GROUP = 2 * KR + 2
DEPTH = 5 * B
GATHER_VMEM = 40 * 1024 * 1024
UPDATE_VMEM = 16 * 1024 * 1024


def split2(x):
    high = x.astype(BF16)
    return high, (x - high.astype(F32)).astype(BF16)


def split3(x):
    high = x.astype(BF16)
    rest = x - high.astype(F32)
    mid = rest.astype(BF16)
    low = (rest - mid.astype(F32)).astype(BF16)
    return high, mid, low


def left4(x):
    h, m = split2(x)
    return jnp.concatenate([h, h, m, m], axis=1)


def right4(x):
    h, m = split2(x)
    return jnp.concatenate([h, m, h, m], axis=1)


def left6(x, axis=1):
    h, m, l = split3(x)
    return jnp.concatenate([h, h, m, h, m, l], axis=axis)


def right6(x, axis=1):
    h, m, l = split3(x)
    return jnp.concatenate([h, m, h, l, m, h], axis=axis)


def dot_nt(a, b):
    return lax.dot_general(a, b, (((1,), (1,)), ((), ())), preferred_element_type=F32)


def operand(points, is_left):
    h, m = split2(points)
    rounded = h.astype(F32) + m.astype(F32)
    half = -0.5 * jnp.sum(rounded * rounded, axis=1, keepdims=True)
    pieces = [jnp.broadcast_to(v.astype(F32), points.shape) for v in split3(half)]
    lane = lax.broadcasted_iota(jnp.int32, points.shape, 1)
    first = 3 if is_left else 0
    extra = jnp.where(lane < 6, 1.0, 0.0)
    for i, piece in enumerate(pieces):
        extra = jnp.where(lane == first + i, piece, extra)
    extra = extra.astype(BF16)
    if is_left:
        return jnp.concatenate([h, h, m, m, extra], axis=1)
    return jnp.concatenate([h, m, h, m, extra], axis=1)


def eliminate(w_ref, dv_ref):
    size = 16
    lane = lax.broadcasted_iota(jnp.int32, (size, B), 1)
    row = lax.broadcasted_iota(jnp.int32, (size, B), 0)
    for start in range(0, B, size):
        rows = slice(start, start + size)
        left = w_ref[rows, 0:B]
        right = w_ref[rows, B : 2 * B]
        cols = [jnp.broadcast_to(left[:, start + k : start + k + 1], (size, B)) for k in range(size)]
        inv = jnp.zeros((size, B), F32)
        for k in range(size):
            rinv = 1.0 / jnp.broadcast_to(cols[k][k : k + 1, :], (size, B))
            inv = jnp.where(row == k, rinv, inv)
            mult = jnp.where(row > k, cols[k] * rinv, 0.0)
            for j in range(k + 1, size):
                cols[j] = cols[j] - mult * cols[j][k : k + 1, :]
            left = left - mult * left[k : k + 1, :]
            right = right - mult * right[k : k + 1, :]
        w_ref[rows, 0:B] = left
        w_ref[rows, B : 2 * B] = right
        dv_ref[rows, :] = inv
        end = start + size
        if end < B:
            scaled = jnp.where(lane >= end, left * inv, 0.0)
            update = lax.dot_general(
                left6(scaled, 0),
                right6(jnp.concatenate([left, right], axis=1), 0),
                (((0,), (0,)), ((), ())),
                preferred_element_type=F32,
            )
            w_ref[end:, :] = w_ref[end:, :] - update[end:, :]


def gather_kernel(
    step_ref,
    feat_ref,
    ls_hbm,
    noise_hbm,
    comp_ref,
    covar_ref,
    mrow_ref,
    colc_ref,
    pf_ref,
    ls_ref,
    noise_ref,
    comp_0,
    comp_1,
    comp_2,
    comp_3,
    feat_v,
    s_a,
    r_a,
    s_b,
    r_b,
    s_f,
    r_f,
    group,
    z_a,
    y_a,
    diag,
    ybuf,
    colcat,
    rowcat,
    rowc,
    w_v,
    dv_v,
    local_sem,
    send_sem,
    recv_sem,
):
    r = lax.axis_index("row")
    c = lax.axis_index("col")
    z = lax.rem(r, NZ)
    y = lax.div(r, NZ)
    axes = {
        "x": (c, NC, lambda i: (r, i)),
        "z": (z, NZ, lambda i: (y * NZ + i, c)),
        "y": (y, NY, lambda i: (i * NZ + z, c)),
    }
    sibling = c + 1 - 2 * lax.rem(c, 2)
    shifts = ((4, 3), (1, 2), (0, 7), (6, 5))

    def shift_of(chips, core):
        total = 0
        for e in range(4):
            for h in range(2):
                total = total + jnp.where(jnp.logical_and(chips == e, core == h), shifts[e][h], 0)
        return total

    def part_at(shift, plane):
        total = 0
        for e in range(4):
            for h in range(2):
                part = lax.rem(lax.div(plane, 2) + e, 4) * 2 + h
                total = total + jnp.where(shift == shifts[e][h], part, 0)
        return total

    chips = lax.rem(lax.div(c, 2) + 4 - lax.div(z, 2), 4)
    to_row = lax.rem(z + shift_of(chips, lax.rem(c, 2)), NZ)
    target = (y * NZ + to_row, z)
    source_part = part_at(lax.rem(z + NZ - c, NZ), c)
    source = (y * NZ + c, source_part)
    far_rows = (3, 5)
    far_parts = {rel: part_at(lax.rem(z + rel + NZ - c, NZ), c) for rel in far_rows}
    far_local = {rel: jnp.logical_and(z == c, far_parts[rel] == c) for rel in far_rows}
    far_targets = {rel: lax.rem(to_row + NZ - rel, NZ) for rel in far_rows}
    far = {8: (4, 3, 5, 2, 6, 1, 7), 4: (2, 1, 3)}
    near = {8: (1, 7, 2, 6, 3, 5, 4), 4: (1, 3, 2)}

    def other(me, d, n):
        return lax.rem(me + d, n)

    comp_v = (comp_0, comp_1, comp_2, comp_3)
    comp_copies = [
        pltpu.make_async_copy(comp_ref.at[pl.ds(k * B * KC, B * KC)], comp_v[k], local_sem.at[4 + k])
        for k in range(KR)
    ]
    feat_copy = pltpu.make_async_copy(feat_ref, feat_v, local_sem.at[0])
    ls_copy = pltpu.make_async_copy(ls_hbm, ls_ref, local_sem.at[1])
    noise_copy = pltpu.make_async_copy(noise_hbm, noise_ref, local_sem.at[2])
    for copy in comp_copies:
        copy.start()
    feat_copy.start()
    ls_copy.start()
    noise_copy.start()

    barrier = pltpu.get_barrier_semaphore()
    for me, n, dev in axes.values():
        for d in far[n]:
            pl.semaphore_signal(barrier, inc=1, device_id=dev(other(me, d, n)), device_id_type=MESH)

    pl.semaphore_signal(barrier, inc=1, device_id=source, device_id_type=MESH)
    pl.semaphore_signal(barrier, inc=1, device_id=target, device_id_type=MESH)
    for rel in far_rows:

        @pl.when(jnp.logical_not(far_local[rel]))
        def _(rel=rel):
            pl.semaphore_signal(
                barrier, inc=1, device_id=(y * NZ + c, far_parts[rel]), device_id_type=MESH
            )

    def remote(src, dst, send, recv, dev):
        return pltpu.make_async_remote_copy(
            src_ref=src,
            dst_ref=dst,
            send_sem=send_sem.at[send],
            recv_sem=recv_sem.at[recv],
            device_id=dev,
            device_id_type=MESH,
        )

    waits = []

    def post(copy):
        copy.start()
        waits.append(copy)

    def spread(axis, src, dst, off, order=far):
        me, n, dev = axes[axis]
        for d in order[n]:
            peer = other(me, d, n)
            post(remote(src(peer), dst(me), off + d, off + me, dev(peer)))

    def arrived(axis, dst, off, steps=None):
        me, n, dev = axes[axis]
        for d in steps or near[n]:
            peer = other(me, d, n)
            remote(dst(peer), dst(peer), off + d, off + peer, dev(peer)).wait_recv()

    p = step_ref[0]
    panel_m = lax.div(p, NC)
    panel_c = lax.rem(p, NC)
    panel_k = lax.div(p, NR)
    panel_r = lax.rem(p, NR)
    panel_z = lax.rem(panel_r, NZ)
    panel_y = lax.div(panel_r, NZ)

    for k in range(KR):
        comp_copies[k].wait()
        block = comp_v[k][pl.ds(panel_m, B, stride=KC), :]
        s_b[:, k] = block.reshape(NC, PART, B)
    s_a[...] = s_b[:, panel_k]
    r_a[c] = s_a[c]
    r_b[c] = s_b[c]

    alone = jnp.logical_and(z == c, lax.rem(c, 2) == 1)

    @pl.when(jnp.logical_not(alone))
    def _():
        pl.semaphore_wait(barrier, 2 * NC + NY + 1)

    @pl.when(alone)
    def _():
        pl.semaphore_wait(barrier, 2 * NC + NY)

    spread("x", lambda i: s_a.at[i], lambda i: r_a.at[i], 0)
    spread("x", lambda i: s_b.at[i], lambda i: r_b.at[i], 8)
    feat_copy.wait()
    ls_copy.wait()
    noise_copy.wait()

    part = pl.ds(pl.multiple_of(source_part * PART, PART), PART)
    feat_out = remote(feat_v.at[:, y, part, :], group.at[source_part, 6:10], 24, 24, source)
    feat_in = remote(feat_v.at[:, y, part, :], group.at[c, 6:10], 24, 24, source)
    post(feat_out)

    inv_ls = 1.0 / ls_ref[...]
    feat_p = feat_v[lax.div(panel_m, 4), lax.rem(panel_m, 4)] * inv_ls
    s_f[:, 0] = feat_p.reshape(NC, PART, B)
    noise_p = noise_ref[pl.ds(panel_m, 1), :]
    s_f[:, 1] = jnp.broadcast_to(noise_p.reshape(1, 1, B), (NC, PART, B))
    r_f[c] = s_f[c]
    spread("x", lambda i: s_f.at[i], lambda i: r_f.at[i], 16)

    def prepare(m, carry):
        pts = feat_v[lax.div(m, 4), lax.rem(m, 4)] * inv_ls
        colcat[pl.ds(pl.multiple_of(m * B, B), B), :] = operand(pts, False)
        return carry

    lax.fori_loop(0, KC // 2, prepare, 0, unroll=4)

    arrived("x", lambda i: r_a.at[i], 0)
    z_a[z] = r_a[panel_c]
    spread("z", lambda i: z_a.at[z], lambda i: z_a.at[i], 32)

    arrived("x", lambda i: r_b.at[i], 8)
    group[c, 0:4] = r_b[panel_c]
    move = remote(group.at[c, 0:4], ybuf.at[0, 0], 25, 25, target)
    post(move)
    far_moves = []
    for rel in far_rows:
        far_move = remote(
            group.at[c, 0:4], ybuf.at[rel, 0], 40 + rel, 40 + rel, (y * NZ + far_targets[rel], z)
        )
        stays = jnp.logical_and(z == c, far_targets[rel] == z)
        far_moves.append((far_move, stays))

        @pl.when(jnp.logical_not(stays))
        def _(far_move=far_move):
            far_move.start()

        @pl.when(stays)
        def _(rel=rel):
            ybuf[rel, 0] = group[c, 0:4]

    def over_y(rel):
        for d in near[NY]:
            peer = other(y, d, NY)
            slot = NY - d
            post(
                remote(
                    ybuf.at[rel, 0], ybuf.at[rel, slot], 64 + rel * 4 + d, 64 + rel * 4 + slot, axes["y"][2](peer)
                )
            )

    def from_y(rel):
        for d in near[NY]:
            here = ybuf.at[rel, d]
            remote(here, here, 64, 64 + rel * 4 + d, axes["y"][2](other(y, d, NY))).wait_recv()

    def over_z(d):
        post(remote(ybuf.at[0, 0], ybuf.at[NZ - d, 0], 40 + d, 40 + NZ - d, axes["z"][2](other(z, d, NZ))))

    def over_z4(slot):
        post(remote(ybuf.at[0, slot], ybuf.at[4, slot], 96 + slot, 96 + slot, axes["z"][2](other(z, 4, NZ))))

    def from_z(d):
        here = ybuf.at[d, 0]
        landed = remote(here, here, 40, 40 + d, axes["z"][2](other(z, d, NZ)))
        if d not in far_rows:
            landed.wait_recv()
            return

        @pl.when(jnp.logical_not(far_local[d]))
        def _():
            landed.wait_recv()

    arrived("x", lambda i: r_f.at[i], 16)
    group[c, 4:6] = r_f[panel_c]
    feat_in.wait_recv()

    mates = [(0, sibling)] + [(d, other(c, d, NC)) for d in (2, 6, 4)]
    for d, peer in mates[1:] + mates[:1]:
        post(remote(group.at[c], group.at[c], 120 + d, 120 + c, (r, peer)))
    lax.fori_loop(KC // 2, KC, prepare, 0, unroll=4)

    arrived("z", lambda i: z_a.at[i], 32)
    y_a[y] = z_a[panel_z]
    spread("y", lambda i: y_a.at[y], lambda i: y_a.at[i], 48)

    move.wait_recv()
    for d in (1, 7, 2, 6, 4):
        over_z(d)
    over_y(0)

    for d, peer in mates[1:]:
        slot = group.at[peer]
        remote(slot, slot, 120 + d, 120 + peer, (r, peer)).wait_recv()
        post(remote(slot, slot, 121 + d, 120 + peer, (r, sibling)))

    arrived("y", lambda i: y_a.at[i], 48)
    diag[c] = y_a[panel_y]
    spread("x", lambda i: diag.at[c], lambda i: diag.at[i], 56)

    def relay(*rels):
        for rel in rels:
            from_z(rel)
            over_y(rel)

    relay(1, 7)
    for d in (0, 2, 6, 4):
        slot = group.at[other(sibling, d, NC)]
        remote(slot, slot, 120, 120 + other(sibling, d, NC), (r, sibling)).wait_recv()

    for k in range(KR):
        rows = group[:, 6 + k].reshape(B, B)
        rowcat[k * B : (k + 1) * B, :] = operand(rows * inv_ls, True)
    eye = lax.broadcasted_iota(jnp.int32, (B, B), 0) == lax.broadcasted_iota(jnp.int32, (B, B), 1)

    def cover(quarter):
        for m2 in (2 * quarter, 2 * quarter + 1):
            expo = dot_nt(rowcat[...], colcat[m2 * 2 * B : (m2 + 1) * 2 * B, :])
            for j in range(2):
                m = m2 * 2 + j
                for k in range(KR):
                    value = jnp.exp(expo[k * B : (k + 1) * B, j * B : (j + 1) * B])
                    value = value + comp_v[k][pl.ds(m, B, stride=KC), :]
                    if m // 4 == k:
                        same = jnp.logical_and(z == c, y == m % 4)
                        value = value + jnp.where(jnp.logical_and(eye, same), noise_ref[m : m + 1, :], 0.0)
                    covar_ref[m, k * B : (k + 1) * B, :] = value

    cover(0)
    from_y(0)
    for slot in range(1, NY):
        over_z4(slot)
    relay(3, 5)
    relay(2, 6)
    cover(1)
    cover(2)

    pts_p = group[:, 4].reshape(B, B)
    left_p, right_p = operand(pts_p, True), operand(pts_p, False)
    noise_p = jnp.where(eye, group[0, 5, 0:1, :], 0.0)
    kernel_p = jnp.exp(dot_nt(left_p, right_p)) + noise_p
    kernel_row = jnp.exp(dot_nt(rowcat[...], right_p))
    for k in range(KR):
        here = k * NR + r == p
        raw = group[:, k].reshape(B, B)
        value = kernel_row[k * B : (k + 1) * B, :] + raw + jnp.where(here, noise_p, 0.0)
        rowc[k * B : (k + 1) * B, :] = left6(value)

    arrived("x", lambda i: diag.at[i], 56)
    w_v[:, 0:B] = kernel_p + diag[...].reshape(B, B)
    w_v[:, B : 2 * B] = jnp.where(eye, 1.0, 0.0)

    eliminate(w_v, dv_v)
    linv = w_v[:, B : 2 * B] * jnp.sqrt(dv_v[...])
    dv_v[...] = linv
    inverse = lax.dot_general(
        left6(linv, 0), right6(linv, 0), (((0,), (0,)), ((), ())), preferred_element_type=F32
    )
    weights = dot_nt(rowc[...], right6(inverse))
    share = right6(dv_v[pl.ds(pl.multiple_of(c * PART, PART), PART), :])
    mine = dot_nt(share, rowc[...])
    row = lax.broadcasted_iota(jnp.int32, (PART, B), 1)
    col = lax.broadcasted_iota(jnp.int32, (PART, B), 0) + c * PART
    for k in range(KR):
        w = k * NR + r
        mrow_ref[k * B : (k + 1) * B, :] = jnp.where(w > p, weights[k * B : (k + 1) * B, :], 0.0)
        keep = jnp.logical_or(w > p, jnp.logical_and(w == p, col <= row))
        pf_ref[k] = jnp.where(keep, mine[:, k * B : (k + 1) * B], 0.0)

    for quarter in range(4):
        rows = slice(quarter * 4 * B, (quarter + 1) * 4 * B)
        colc_ref[rows, :] = jnp.exp(dot_nt(colcat[rows, :], left_p))
    cover(3)

    for rel in (1, 7, 2, 6, 3, 5):
        from_y(rel)
    from_z(4)
    for slot in range(1, NY):
        far_z = ybuf.at[4, slot]
        remote(far_z, far_z, 96, 96 + slot, axes["z"][2](other(z, 4, NZ))).wait_recv()
    places = [
        lax.rem(c + shift_of(lax.rem(i // 2 + 4 - lax.div(c, 2), 4), i % 2) + NZ - z, NZ) for i in range(NC)
    ]
    for rel in range(NY):
        for k in range(KR):
            m = k * 4 + other(y, rel, NY)
            raw = jnp.concatenate([ybuf[place, rel, k] for place in places], axis=0)
            rows = pl.ds(pl.multiple_of(m * B, B), B)
            colc_ref[rows, :] = jnp.where(m * NC + c > p, colc_ref[rows, :] + raw, 0.0)

    for copy in waits:
        copy.wait_send()
    for far_move, stays in far_moves:

        @pl.when(jnp.logical_not(stays))
        def _(far_move=far_move):
            far_move.wait_send()


def update_kernel(covar_ref, mrow_ref, colc_ref, pf_in, out_ref, pf_ref, out_v, sem):
    left = left4(mrow_ref[...])
    copies = []
    for half in range(2):
        for pair in range(2):
            rows = slice(pair * 2 * B, (pair + 1) * 2 * B)
            for m2 in range(half * 4, half * 4 + 4):
                update = dot_nt(left[rows, :], right4(colc_ref[m2 * 2 * B : (m2 + 1) * 2 * B, :]))
                for j in range(2):
                    m = m2 * 2 + j
                    value = covar_ref[m, rows, :] - update[:, j * B : (j + 1) * B]
                    out_v[pl.ds(pair * 2 * B * KC + m, 2 * B, stride=KC), :] = value
            view = out_v.reshape(KR * B, KC, B)
            part = (pl.ds(pair * 2 * B, 2 * B), pl.ds(half * 8, 8))
            copy = pltpu.make_async_copy(view.at[part], out_ref.at[part], sem.at[half * 2 + pair])
            copy.start()
            copies.append(copy)
    pf_ref[...] = pf_in[...]
    for copy in copies:
        copy.wait()


def in_hbm(x):
    return pltpu.with_memory_space_constraint(x, pltpu.HBM)


def body(features, lengthscales, noise_var, component, step_index):
    hbm = pl.BlockSpec(memory_space=pltpu.HBM)
    vmem = pl.BlockSpec(memory_space=pltpu.VMEM)
    smem = pl.BlockSpec(memory_space=pltpu.SMEM)
    covar, mrow, colc, pf = pl.pallas_call(
        gather_kernel,
        out_shape=(
            jax.ShapeDtypeStruct((KC, KR * B, B), F32),
            jax.ShapeDtypeStruct((KR * B, B), F32),
            jax.ShapeDtypeStruct((KC * B, B), F32),
            jax.ShapeDtypeStruct((KR, PART, B), F32),
        ),
        in_specs=[smem, hbm, hbm, hbm, hbm],
        out_specs=(vmem, vmem, vmem, vmem),
        scratch_shapes=[
            pltpu.VMEM((1, B), F32),
            pltpu.VMEM((KC, B), F32),
            pltpu.VMEM((B * KC, B), F32),
            pltpu.VMEM((B * KC, B), F32),
            pltpu.VMEM((B * KC, B), F32),
            pltpu.VMEM((B * KC, B), F32),
            pltpu.VMEM((4, 4, B, B), F32),
            pltpu.VMEM((NC, PART, B), F32),
            pltpu.VMEM((NC, PART, B), F32),
            pltpu.VMEM((NC, KR, PART, B), F32),
            pltpu.VMEM((NC, KR, PART, B), F32),
            pltpu.VMEM((NC, 2, PART, B), F32),
            pltpu.VMEM((NC, 2, PART, B), F32),
            pltpu.VMEM((NC, GROUP, PART, B), F32),
            pltpu.VMEM((NZ, PART, B), F32),
            pltpu.VMEM((NY, PART, B), F32),
            pltpu.VMEM((NC, PART, B), F32),
            pltpu.VMEM((NZ, NY, KR, PART, B), F32),
            pltpu.VMEM((KC * B, DEPTH), BF16),
            pltpu.VMEM((KR * B, DEPTH), BF16),
            pltpu.VMEM((KR * B, 6 * B), BF16),
            pltpu.VMEM((B, 2 * B), F32),
            pltpu.VMEM((B, B), F32),
            pltpu.SemaphoreType.DMA((8,)),
            pltpu.SemaphoreType.DMA((136,)),
            pltpu.SemaphoreType.DMA((136,)),
        ],
        compiler_params=pltpu.CompilerParams(
            collective_id=0, has_side_effects=True, vmem_limit_bytes=GATHER_VMEM
        ),
        name="gather_panel",
    )(
        step_index,
        in_hbm(features.reshape(4, 4, B, B)),
        in_hbm(lengthscales.reshape(1, B)),
        in_hbm(noise_var),
        in_hbm(component.reshape(KR * B * KC, B)),
    )
    trailing, pf = pl.pallas_call(
        update_kernel,
        out_shape=(
            jax.ShapeDtypeStruct((KR * B, KC, B), F32),
            jax.ShapeDtypeStruct((KR, PART, B), F32),
        ),
        in_specs=[vmem, vmem, vmem, vmem],
        out_specs=(hbm, vmem),
        scratch_shapes=[
            pltpu.VMEM((KR * B * KC, B), F32),
            pltpu.SemaphoreType.DMA((4,)),
        ],
        compiler_params=pltpu.CompilerParams(vmem_limit_bytes=UPDATE_VMEM),
        name="update_blocks",
    )(covar, mrow, colc, pf)
    return jnp.swapaxes(pf, 1, 2), trailing.reshape(KR, B, KC, B)


def solution(mesh):
    in_specs = (P(None, "col", None), P(), P(None, "col"), P(None, "row", None, "col"), P())
    out_specs = (P(None, "row", "col"), P(None, "row", None, "col"))
    return jax.shard_map(body, mesh=mesh, in_specs=in_specs, out_specs=out_specs, check_vma=False)
```

```python
import functools

import jax
import jax.numpy as jnp
from jax import lax
from jax.experimental import pallas as pl
from jax.experimental.pallas import tpu as pltpu
from jax.sharding import PartitionSpec as P

MESH = pl.DeviceIdType.MESH
F32 = jnp.float32
BF16 = jnp.bfloat16
B = 128
KR, KC, NR, NC = 4, 16, 32, 8
NY, NZ = 4, 8
PART = B // NC
GROUP = 2 * KR + 2
DEPTH = 5 * B
GATHER_VMEM = 40 * 1024 * 1024
UPDATE_VMEM = 16 * 1024 * 1024


def split2(x):
    high = x.astype(BF16)
    return high, (x - high.astype(F32)).astype(BF16)


def split3(x):
    high = x.astype(BF16)
    rest = x - high.astype(F32)
    mid = rest.astype(BF16)
    low = (rest - mid.astype(F32)).astype(BF16)
    return high, mid, low


def left4(x):
    h, m = split2(x)
    return jnp.concatenate([h, h, m, m], axis=1)


def right4(x):
    h, m = split2(x)
    return jnp.concatenate([h, m, h, m], axis=1)


def left6(x, axis=1):
    h, m, l = split3(x)
    return jnp.concatenate([h, h, m, h, m, l], axis=axis)


def right6(x, axis=1):
    h, m, l = split3(x)
    return jnp.concatenate([h, m, h, l, m, h], axis=axis)


def dot_nt(a, b):
    return lax.dot_general(a, b, (((1,), (1,)), ((), ())), preferred_element_type=F32)


def operand(points, is_left):
    h, m = split2(points)
    rounded = h.astype(F32) + m.astype(F32)
    half = -0.5 * jnp.sum(rounded * rounded, axis=1, keepdims=True)
    pieces = [jnp.broadcast_to(v.astype(F32), points.shape) for v in split3(half)]
    lane = lax.broadcasted_iota(jnp.int32, points.shape, 1)
    first = 3 if is_left else 0
    extra = jnp.where(lane < 6, 1.0, 0.0)
    for i, piece in enumerate(pieces):
        extra = jnp.where(lane == first + i, piece, extra)
    extra = extra.astype(BF16)
    if is_left:
        return jnp.concatenate([h, h, m, m, extra], axis=1)
    return jnp.concatenate([h, m, h, m, extra], axis=1)


def eliminate(w_ref, dv_ref, between):
    size = 16
    lane = lax.broadcasted_iota(jnp.int32, (size, B), 1)
    row = lax.broadcasted_iota(jnp.int32, (size, B), 0)
    for start in range(0, B, size):
        rows = slice(start, start + size)
        left = w_ref[rows, 0:B]
        right = w_ref[rows, B : 2 * B]
        cols = [jnp.broadcast_to(left[:, start + k : start + k + 1], (size, B)) for k in range(size)]
        inv = jnp.zeros((size, B), F32)
        for k in range(size):
            rinv = 1.0 / jnp.broadcast_to(cols[k][k : k + 1, :], (size, B))
            inv = jnp.where(row == k, rinv, inv)
            mult = jnp.where(row > k, cols[k] * rinv, 0.0)
            for j in range(k + 1, size):
                cols[j] = cols[j] - mult * cols[j][k : k + 1, :]
            left = left - mult * left[k : k + 1, :]
            right = right - mult * right[k : k + 1, :]
        w_ref[rows, 0:B] = left
        w_ref[rows, B : 2 * B] = right
        dv_ref[rows, :] = inv
        end = start + size
        if end < B:
            scaled = jnp.where(lane >= end, left * inv, 0.0)
            update = lax.dot_general(
                left6(scaled, 0),
                right6(jnp.concatenate([left, right], axis=1), 0),
                (((0,), (0,)), ((), ())),
                preferred_element_type=F32,
            )
            w_ref[end:, :] = w_ref[end:, :] - update[end:, :]
        between(end // size)


def gather_kernel(
    step_ref,
    feat_ref,
    ls_hbm,
    noise_hbm,
    comp_ref,
    covar_ref,
    mrow_ref,
    colc_ref,
    pf_ref,
    ls_ref,
    noise_ref,
    comp_0,
    comp_1,
    comp_2,
    comp_3,
    feat_v,
    s_a,
    r_a,
    s_b,
    r_b,
    s_f,
    r_f,
    group,
    z_a,
    y_a,
    diag,
    ybuf,
    colcat,
    rowcat,
    rowc,
    w_v,
    dv_v,
    local_sem,
    send_sem,
    recv_sem,
):
    r = lax.axis_index("row")
    c = lax.axis_index("col")
    z = lax.rem(r, NZ)
    y = lax.div(r, NZ)
    axes = {
        "x": (c, NC, lambda i: (r, i)),
        "z": (z, NZ, lambda i: (y * NZ + i, c)),
        "y": (y, NY, lambda i: (i * NZ + z, c)),
    }
    sibling = c + 1 - 2 * lax.rem(c, 2)
    shifts = ((4, 3), (1, 2), (0, 7), (6, 5))

    def shift_of(chips, core):
        total = 0
        for e in range(4):
            for h in range(2):
                total = total + jnp.where(jnp.logical_and(chips == e, core == h), shifts[e][h], 0)
        return total

    def part_at(shift, plane):
        total = 0
        for e in range(4):
            for h in range(2):
                part = lax.rem(lax.div(plane, 2) + e, 4) * 2 + h
                total = total + jnp.where(shift == shifts[e][h], part, 0)
        return total

    chips = lax.rem(lax.div(c, 2) + 4 - lax.div(z, 2), 4)
    to_row = lax.rem(z + shift_of(chips, lax.rem(c, 2)), NZ)
    target = (y * NZ + to_row, z)
    source_part = part_at(lax.rem(z + NZ - c, NZ), c)
    source = (y * NZ + c, source_part)
    far = {8: (4, 3, 5, 2, 6, 1, 7), 4: (2, 1, 3)}
    near = {8: (1, 7, 2, 6, 3, 5, 4), 4: (1, 3, 2)}

    def other(me, d, n):
        return lax.rem(me + d, n)

    comp_v = (comp_0, comp_1, comp_2, comp_3)
    comp_copies = [
        pltpu.make_async_copy(comp_ref.at[pl.ds(k * B * KC, B * KC)], comp_v[k], local_sem.at[4 + k])
        for k in range(KR)
    ]
    feat_copy = pltpu.make_async_copy(feat_ref, feat_v, local_sem.at[0])
    ls_copy = pltpu.make_async_copy(ls_hbm, ls_ref, local_sem.at[1])
    noise_copy = pltpu.make_async_copy(noise_hbm, noise_ref, local_sem.at[2])
    for copy in comp_copies:
        copy.start()
    feat_copy.start()
    ls_copy.start()
    noise_copy.start()

    barrier = pltpu.get_barrier_semaphore()
    for me, n, dev in axes.values():
        for d in far[n]:
            pl.semaphore_signal(barrier, inc=1, device_id=dev(other(me, d, n)), device_id_type=MESH)

    pl.semaphore_signal(barrier, inc=1, device_id=source, device_id_type=MESH)
    pl.semaphore_signal(barrier, inc=1, device_id=target, device_id_type=MESH)

    def remote(src, dst, send, recv, dev):
        return pltpu.make_async_remote_copy(
            src_ref=src,
            dst_ref=dst,
            send_sem=send_sem.at[send],
            recv_sem=recv_sem.at[recv],
            device_id=dev,
            device_id_type=MESH,
        )

    waits = []

    def post(copy):
        copy.start()
        waits.append(copy)

    def spread(axis, src, dst, off, order=far):
        me, n, dev = axes[axis]
        for d in order[n]:
            peer = other(me, d, n)
            post(remote(src(peer), dst(me), off + d, off + me, dev(peer)))

    def arrived(axis, dst, off, steps=None):
        me, n, dev = axes[axis]
        for d in steps or near[n]:
            peer = other(me, d, n)
            remote(dst(peer), dst(peer), off + d, off + peer, dev(peer)).wait_recv()

    p = step_ref[0]
    panel_m = lax.div(p, NC)
    panel_c = lax.rem(p, NC)
    panel_k = lax.div(p, NR)
    panel_r = lax.rem(p, NR)
    panel_z = lax.rem(panel_r, NZ)
    panel_y = lax.div(panel_r, NZ)

    for k in range(KR):
        comp_copies[k].wait()
        block = comp_v[k][pl.ds(panel_m, B, stride=KC), :]
        s_b[:, k] = block.reshape(NC, PART, B)
    s_a[...] = s_b[:, panel_k]
    r_a[c] = s_a[c]
    r_b[c] = s_b[c]

    pl.semaphore_wait(barrier, 2 * NC + NY - 1)

    spread("x", lambda i: s_a.at[i], lambda i: r_a.at[i], 0)
    spread("x", lambda i: s_b.at[i], lambda i: r_b.at[i], 8)
    feat_copy.wait()
    ls_copy.wait()
    noise_copy.wait()

    part = pl.ds(pl.multiple_of(source_part * PART, PART), PART)
    feat_out = remote(feat_v.at[:, y, part, :], group.at[source_part, 6:10], 24, 24, source)
    feat_in = remote(feat_v.at[:, y, part, :], group.at[c, 6:10], 24, 24, source)
    post(feat_out)

    inv_ls = 1.0 / ls_ref[...]
    feat_p = feat_v[lax.div(panel_m, 4), lax.rem(panel_m, 4)] * inv_ls
    s_f[:, 0] = feat_p.reshape(NC, PART, B)
    noise_p = noise_ref[pl.ds(panel_m, 1), :]
    s_f[:, 1] = jnp.broadcast_to(noise_p.reshape(1, 1, B), (NC, PART, B))
    r_f[c] = s_f[c]
    spread("x", lambda i: s_f.at[i], lambda i: r_f.at[i], 16)

    def prepare(m, carry):
        pts = feat_v[lax.div(m, 4), lax.rem(m, 4)] * inv_ls
        colcat[pl.ds(pl.multiple_of(m * B, B), B), :] = operand(pts, False)
        return carry

    lax.fori_loop(0, KC // 2, prepare, 0, unroll=4)

    arrived("x", lambda i: r_a.at[i], 0)
    z_a[z] = r_a[panel_c]
    spread("z", lambda i: z_a.at[z], lambda i: z_a.at[i], 32)

    arrived("x", lambda i: r_b.at[i], 8)
    group[c, 0:4] = r_b[panel_c]
    move = remote(group.at[c, 0:4], ybuf.at[0, 0], 25, 25, target)
    post(move)

    def over_y(rel):
        for d in near[NY]:
            peer = other(y, d, NY)
            slot = NY - d
            post(
                remote(
                    ybuf.at[rel, 0], ybuf.at[rel, slot], 64 + rel * 4 + d, 64 + rel * 4 + slot, axes["y"][2](peer)
                )
            )

    def from_y(rel):
        for d in near[NY]:
            here = ybuf.at[rel, d]
            remote(here, here, 64, 64 + rel * 4 + d, axes["y"][2](other(y, d, NY))).wait_recv()

    def over_z(d):
        post(remote(ybuf.at[0, 0], ybuf.at[NZ - d, 0], 40 + d, 40 + NZ - d, axes["z"][2](other(z, d, NZ))))

    def over_z4(slot):
        post(remote(ybuf.at[0, slot], ybuf.at[4, slot], 96 + slot, 96 + slot, axes["z"][2](other(z, 4, NZ))))

    def from_z(d):
        here = ybuf.at[d, 0]
        remote(here, here, 40, 40 + d, axes["z"][2](other(z, d, NZ))).wait_recv()

    arrived("x", lambda i: r_f.at[i], 16)
    group[c, 4:6] = r_f[panel_c]
    feat_in.wait_recv()

    mates = [(0, sibling)] + [(d, other(c, d, NC)) for d in (2, 6, 4)]
    for d, peer in mates[1:] + mates[:1]:
        post(remote(group.at[c], group.at[c], 120 + d, 120 + c, (r, peer)))
    lax.fori_loop(KC // 2, KC, prepare, 0, unroll=4)

    arrived("z", lambda i: z_a.at[i], 32)
    y_a[y] = z_a[panel_z]
    spread("y", lambda i: y_a.at[y], lambda i: y_a.at[i], 48)

    move.wait_recv()
    for d in near[NZ][:4]:
        over_z(d)
    over_y(0)
    for d in near[NZ][4:]:
        over_z(d)

    for d, peer in mates[1:]:
        slot = group.at[peer]
        remote(slot, slot, 120 + d, 120 + peer, (r, peer)).wait_recv()
        post(remote(slot, slot, 121 + d, 120 + peer, (r, sibling)))

    arrived("y", lambda i: y_a.at[i], 48)
    diag[c] = y_a[panel_y]
    spread("x", lambda i: diag.at[c], lambda i: diag.at[i], 56)

    def relay(*rels):
        for rel in rels:
            from_z(rel)
            over_y(rel)

    relay(1, 7)
    for d in (0, 2, 6, 4):
        slot = group.at[other(sibling, d, NC)]
        remote(slot, slot, 120, 120 + other(sibling, d, NC), (r, sibling)).wait_recv()

    for k in range(KR):
        rows = group[:, 6 + k].reshape(B, B)
        rowcat[k * B : (k + 1) * B, :] = operand(rows * inv_ls, True)
    eye = lax.broadcasted_iota(jnp.int32, (B, B), 0) == lax.broadcasted_iota(jnp.int32, (B, B), 1)

    def cover(quarter):
        for m2 in (2 * quarter, 2 * quarter + 1):
            expo = dot_nt(rowcat[...], colcat[m2 * 2 * B : (m2 + 1) * 2 * B, :])
            for j in range(2):
                m = m2 * 2 + j
                for k in range(KR):
                    value = jnp.exp(expo[k * B : (k + 1) * B, j * B : (j + 1) * B])
                    value = value + comp_v[k][pl.ds(m, B, stride=KC), :]
                    if m // 4 == k:
                        same = jnp.logical_and(z == c, y == m % 4)
                        value = value + jnp.where(jnp.logical_and(eye, same), noise_ref[m : m + 1, :], 0.0)
                    covar_ref[m, k * B : (k + 1) * B, :] = value

    cover(0)
    from_y(0)
    for slot in range(1, NY):
        over_z4(slot)
    relay(2, 6)
    cover(1)
    cover(2)

    pts_p = group[:, 4].reshape(B, B)
    left_p, right_p = operand(pts_p, True), operand(pts_p, False)
    noise_p = jnp.where(eye, group[0, 5, 0:1, :], 0.0)
    kernel_p = jnp.exp(dot_nt(left_p, right_p)) + noise_p
    kernel_row = jnp.exp(dot_nt(rowcat[...], right_p))
    for k in range(KR):
        here = k * NR + r == p
        raw = group[:, k].reshape(B, B)
        value = kernel_row[k * B : (k + 1) * B, :] + raw + jnp.where(here, noise_p, 0.0)
        rowc[k * B : (k + 1) * B, :] = left6(value)

    arrived("x", lambda i: diag.at[i], 56)
    w_v[:, 0:B] = kernel_p + diag[...].reshape(B, B)
    w_v[:, B : 2 * B] = jnp.where(eye, 1.0, 0.0)

    def between(done):
        if done == 2:
            relay(3, 5)

    eliminate(w_v, dv_v, between)
    linv = w_v[:, B : 2 * B] * jnp.sqrt(dv_v[...])
    dv_v[...] = linv
    inverse = lax.dot_general(
        left6(linv, 0), right6(linv, 0), (((0,), (0,)), ((), ())), preferred_element_type=F32
    )
    weights = dot_nt(rowc[...], right6(inverse))
    share = right6(dv_v[pl.ds(pl.multiple_of(c * PART, PART), PART), :])
    mine = dot_nt(share, rowc[...])
    row = lax.broadcasted_iota(jnp.int32, (PART, B), 1)
    col = lax.broadcasted_iota(jnp.int32, (PART, B), 0) + c * PART
    for k in range(KR):
        w = k * NR + r
        mrow_ref[k * B : (k + 1) * B, :] = jnp.where(w > p, weights[k * B : (k + 1) * B, :], 0.0)
        keep = jnp.logical_or(w > p, jnp.logical_and(w == p, col <= row))
        pf_ref[k] = jnp.where(keep, mine[:, k * B : (k + 1) * B], 0.0)

    for quarter in range(4):
        rows = slice(quarter * 4 * B, (quarter + 1) * 4 * B)
        colc_ref[rows, :] = jnp.exp(dot_nt(colcat[rows, :], left_p))
    cover(3)

    for rel in (1, 7, 2, 6, 3, 5):
        from_y(rel)
    from_z(4)
    for slot in range(1, NY):
        far_z = ybuf.at[4, slot]
        remote(far_z, far_z, 96, 96 + slot, axes["z"][2](other(z, 4, NZ))).wait_recv()
    places = [
        lax.rem(c + shift_of(lax.rem(i // 2 + 4 - lax.div(c, 2), 4), i % 2) + NZ - z, NZ) for i in range(NC)
    ]
    for rel in range(NY):
        for k in range(KR):
            m = k * 4 + other(y, rel, NY)
            raw = jnp.concatenate([ybuf[place, rel, k] for place in places], axis=0)
            rows = pl.ds(pl.multiple_of(m * B, B), B)
            colc_ref[rows, :] = jnp.where(m * NC + c > p, colc_ref[rows, :] + raw, 0.0)

    for copy in waits:
        copy.wait_send()


def update_kernel(covar_ref, mrow_ref, colc_ref, pf_in, out_ref, pf_ref, out_v, sem):
    left = left4(mrow_ref[...])
    copies = []
    for half in range(2):
        for pair in range(2):
            rows = slice(pair * 2 * B, (pair + 1) * 2 * B)
            for m2 in range(half * 4, half * 4 + 4):
                update = dot_nt(left[rows, :], right4(colc_ref[m2 * 2 * B : (m2 + 1) * 2 * B, :]))
                for j in range(2):
                    m = m2 * 2 + j
                    value = covar_ref[m, rows, :] - update[:, j * B : (j + 1) * B]
                    out_v[pl.ds(pair * 2 * B * KC + m, 2 * B, stride=KC), :] = value
            view = out_v.reshape(KR * B, KC, B)
            part = (pl.ds(pair * 2 * B, 2 * B), pl.ds(half * 8, 8))
            copy = pltpu.make_async_copy(view.at[part], out_ref.at[part], sem.at[half * 2 + pair])
            copy.start()
            copies.append(copy)
    pf_ref[...] = pf_in[...]
    for copy in copies:
        copy.wait()


def in_hbm(x):
    return pltpu.with_memory_space_constraint(x, pltpu.HBM)


def body(features, lengthscales, noise_var, component, step_index):
    hbm = pl.BlockSpec(memory_space=pltpu.HBM)
    vmem = pl.BlockSpec(memory_space=pltpu.VMEM)
    smem = pl.BlockSpec(memory_space=pltpu.SMEM)
    covar, mrow, colc, pf = pl.pallas_call(
        gather_kernel,
        out_shape=(
            jax.ShapeDtypeStruct((KC, KR * B, B), F32),
            jax.ShapeDtypeStruct((KR * B, B), F32),
            jax.ShapeDtypeStruct((KC * B, B), F32),
            jax.ShapeDtypeStruct((KR, PART, B), F32),
        ),
        in_specs=[smem, hbm, hbm, hbm, hbm],
        out_specs=(vmem, vmem, vmem, vmem),
        scratch_shapes=[
            pltpu.VMEM((1, B), F32),
            pltpu.VMEM((KC, B), F32),
            pltpu.VMEM((B * KC, B), F32),
            pltpu.VMEM((B * KC, B), F32),
            pltpu.VMEM((B * KC, B), F32),
            pltpu.VMEM((B * KC, B), F32),
            pltpu.VMEM((4, 4, B, B), F32),
            pltpu.VMEM((NC, PART, B), F32),
            pltpu.VMEM((NC, PART, B), F32),
            pltpu.VMEM((NC, KR, PART, B), F32),
            pltpu.VMEM((NC, KR, PART, B), F32),
            pltpu.VMEM((NC, 2, PART, B), F32),
            pltpu.VMEM((NC, 2, PART, B), F32),
            pltpu.VMEM((NC, GROUP, PART, B), F32),
            pltpu.VMEM((NZ, PART, B), F32),
            pltpu.VMEM((NY, PART, B), F32),
            pltpu.VMEM((NC, PART, B), F32),
            pltpu.VMEM((NZ, NY, KR, PART, B), F32),
            pltpu.VMEM((KC * B, DEPTH), BF16),
            pltpu.VMEM((KR * B, DEPTH), BF16),
            pltpu.VMEM((KR * B, 6 * B), BF16),
            pltpu.VMEM((B, 2 * B), F32),
            pltpu.VMEM((B, B), F32),
            pltpu.SemaphoreType.DMA((8,)),
            pltpu.SemaphoreType.DMA((136,)),
            pltpu.SemaphoreType.DMA((136,)),
        ],
        compiler_params=pltpu.CompilerParams(
            collective_id=0, has_side_effects=True, vmem_limit_bytes=GATHER_VMEM
        ),
        name="gather_panel",
    )(
        step_index,
        in_hbm(features.reshape(4, 4, B, B)),
        in_hbm(lengthscales.reshape(1, B)),
        in_hbm(noise_var),
        in_hbm(component.reshape(KR * B * KC, B)),
    )
    trailing, pf = pl.pallas_call(
        update_kernel,
        out_shape=(
            jax.ShapeDtypeStruct((KR * B, KC, B), F32),
            jax.ShapeDtypeStruct((KR, PART, B), F32),
        ),
        in_specs=[vmem, vmem, vmem, vmem],
        out_specs=(hbm, vmem),
        scratch_shapes=[
            pltpu.VMEM((KR * B * KC, B), F32),
            pltpu.SemaphoreType.DMA((4,)),
        ],
        compiler_params=pltpu.CompilerParams(vmem_limit_bytes=UPDATE_VMEM),
        name="update_blocks",
    )(covar, mrow, colc, pf)
    return jnp.swapaxes(pf, 1, 2), trailing.reshape(KR, B, KC, B)


def solution(mesh):
    in_specs = (P(None, "col", None), P(), P(None, "col"), P(None, "row", None, "col"), P())
    out_specs = (P(None, "row", "col"), P(None, "row", None, "col"))
    return jax.shard_map(body, mesh=mesh, in_specs=in_specs, out_specs=out_specs, check_vma=False)
```
